256 devices in a mesh: dp: 8 (over z_hi, y), seq: 32 (over z_lo, x, core).
Axes of the slice: x: 4, y: 4, z: 8 (z_hi: 2, z_lo: 4; z = z_hi * 4 + z_lo), core: 2. Of those that a mesh axis runs over, the one named last changes fastest.
Arguments:
- video: bfloat16 [8, 32, 256, 768], P('dp', 'seq'), may hold values from -6 to 6
- w_qkv_space: bfloat16 [768, 2304], replicated, may hold values from -5.809587 to 5.809587
- w_out_space: bfloat16 [768, 768], replicated, may hold values from -0.21875 to 0.21875
- w_qkv_time: bfloat16 [768, 2304], replicated, may hold values from -5.809587 to 5.809587
- w_out_time: bfloat16 [768, 768], replicated, may hold values from -0.21875 to 0.21875
- grad_out: bfloat16 [8, 32, 256, 768], P('dp', 'seq'), may hold values from -24 to 24
Outputs:
- out_video: bfloat16 [8, 32, 256, 768], P('dp', 'seq')
- grad_video: bfloat16 [8, 32, 256, 768], P('dp', 'seq')
- grad_qkv_space: float32 [768, 2304], P('seq')
- grad_out_space: float32 [768, 768], P('seq')
- grad_qkv_time: float32 [768, 2304], P('seq')
- grad_out_time: float32 [768, 768], P('seq')
The draws below stay inside these ranges and needn't reach their ends.
All inputs are finite; a program needn't handle non-finite values.
Results may differ from the reference program's by a relative error of at most 0.038.
Values may be sent and summed in bfloat16 or wider, within the bound.
A program may use at most 128 MiB of HBM per device.

```python
import math
import jax
import jax.numpy as jnp
from jax import lax

D = 768
HD = 64
FRAMES = 32
P_SIZE = 256
INNER = 768
CLIPS = 8


def draw_w_qkv_space(key, part):
    key = jax.random.fold_in(key, 11)
    base = jax.random.truncated_normal(key, -4.0, 4.0, (D, 3 * INNER), jnp.float32) / math.sqrt(D)
    return base.astype(jnp.bfloat16)


def draw_w_qkv_time(key, part):
    key = jax.random.fold_in(key, 13)
    base = jax.random.truncated_normal(key, -4.0, 4.0, (D, 3 * INNER), jnp.float32) / math.sqrt(D)
    return base.astype(jnp.bfloat16)


def draw_grad_out(key, part):
    key = jax.random.fold_in(key, 17)
    frame_key, place_key, noise_key = jax.random.split(key, 3)
    frame_scale = jnp.exp(jax.random.uniform(frame_key, (CLIPS, FRAMES, 1, 1), jnp.float32, math.log(0.3), math.log(3.0)))
    place_scale = jnp.exp(jax.random.uniform(place_key, (1, 1, P_SIZE, 1), jnp.float32, math.log(0.5), math.log(2.0)))
    noise = jax.random.truncated_normal(noise_key, -4.0, 4.0, (CLIPS, FRAMES, P_SIZE, D), jnp.float32)
    return (noise * frame_scale * place_scale).astype(jnp.bfloat16)


def level_of(own_key, extent, cuts, low, top_value):
    gain = 1.0
    for position, parts in cuts:
        steps = jax.random.uniform(jax.random.fold_in(jax.random.fold_in(own_key, 6), position), (parts,), jnp.float32, low / len(cuts), top_value / len(cuts))
        gain = gain * jnp.repeat(jnp.exp(steps), extent[position] // parts).reshape((-1,) + (1,) * (len(extent) - 1 - position))
    return gain


def scatter_about(own_key, shape, spread, most, cuts=(), held_as=jnp.bfloat16):
    level = level_of(own_key, shape, cuts, -0.22, 0.18) if cuts else 1.0
    result = jax.random.normal(own_key, shape, jnp.float32) * spread * level
    return jnp.minimum(jnp.maximum(result, -most), most).astype(held_as)


def setup_inputs(seed: int = 0) -> dict:
    streams_of = jax.random.split(jax.random.key(seed), 7)
    return {
        "video": scatter_about(streams_of[0], (CLIPS, FRAMES, P_SIZE, D), 1.0, 6.0, ((0, 8), (1, 32))),
        "w_qkv_space": draw_w_qkv_space(jax.random.fold_in(streams_of[6], 71), 0),
        "w_out_space": scatter_about(streams_of[2], (INNER, D), INNER ** -0.5, 0.21875),
        "w_qkv_time": draw_w_qkv_time(jax.random.fold_in(streams_of[6], 71), 0),
        "w_out_time": scatter_about(streams_of[4], (INNER, D), INNER ** -0.5, 0.21875),
        "grad_out": draw_grad_out(jax.random.fold_in(streams_of[6], 71), 0),
    }


epsilon = 1e-05

def forms(time_major):
    if time_major:
        return ('lbhd', 'mbhd')
    return ('blhd', 'bmhd')

def normalize(rows_wide):
    centre_mean = lax.optimization_barrier(jnp.mean(rows_wide, axis=-1, keepdims=True))
    centred = rows_wide - centre_mean
    variance = lax.optimization_barrier(jnp.mean(centred * centred, axis=-1, keepdims=True))
    inverse = lax.rsqrt(variance + epsilon)
    return (centred * inverse, inverse)

def attend(queries, keys_in, values, time_major):
    query_form, key_form = forms(time_major)
    factor = 1.0 / math.sqrt(HD)
    scores = jnp.einsum(query_form + ',' + key_form + '->bhlm', queries.astype(jnp.float32), keys_in.astype(jnp.float32)) * factor
    highest = lax.optimization_barrier(jnp.max(scores, axis=-1, keepdims=True))
    weights = jnp.exp(scores - highest)
    probs_full = weights / lax.optimization_barrier(jnp.sum(weights, axis=-1, keepdims=True))
    probs_low = lax.optimization_barrier(probs_full.astype(jnp.bfloat16))
    attended = jnp.einsum('bhlm,' + key_form + '->' + query_form, probs_low.astype(jnp.float32), values.astype(jnp.float32))
    return (attended.astype(jnp.bfloat16), probs_full, probs_low)

def attend_back(queries, keys_in, values, probs_full, probs_low, d_attended, time_major):
    query_form, key_form = forms(time_major)
    factor = 1.0 / math.sqrt(HD)
    d_wide = d_attended.astype(jnp.float32)
    d_values = jnp.einsum('bhlm,' + query_form + '->' + key_form, probs_low.astype(jnp.float32), d_wide)
    d_probs = jnp.einsum(query_form + ',' + key_form + '->bhlm', d_wide, values.astype(jnp.float32))
    d_scores = probs_full * (d_probs - lax.optimization_barrier(jnp.sum(d_probs * probs_full, axis=-1, keepdims=True))) * factor
    d_queries = jnp.einsum('bhlm,' + key_form + '->' + query_form, d_scores, keys_in.astype(jnp.float32))
    d_keys = jnp.einsum('bhlm,' + query_form + '->' + key_form, d_scores, queries.astype(jnp.float32))
    return (d_queries.astype(jnp.bfloat16), d_keys.astype(jnp.bfloat16), d_values.astype(jnp.bfloat16))

def block_forward(tokens_in, w_qkv, w_out, time_major):
    dim_one, dim_two, feature_count = tokens_in.shape
    head_count = w_out.shape[0] // HD
    rows_wide = tokens_in.reshape(-1, feature_count).astype(jnp.float32)
    normed, _ = normalize(rows_wide)
    normed_low = normed.astype(jnp.bfloat16)
    projected = jnp.dot(normed_low, w_qkv, preferred_element_type=jnp.float32).astype(jnp.bfloat16)
    pieces = projected.reshape(dim_one, dim_two, 3, head_count, HD)
    queries = pieces[:, :, 0]
    keys_in = pieces[:, :, 1]
    values = pieces[:, :, 2]
    attended, probs_full, probs_low = attend(queries, keys_in, values, time_major)
    attended_rows = attended.reshape(-1, w_out.shape[0])
    summed = rows_wide + jnp.dot(attended_rows, w_out, preferred_element_type=jnp.float32)
    output_rows = summed.astype(jnp.bfloat16).reshape(tokens_in.shape)
    return (output_rows, (normed_low, queries, keys_in, values, probs_full, probs_low, attended_rows))

def block_backward(tokens_in, saved, grad_rows, w_qkv, w_out, time_major):
    normed_low, queries, keys_in, values, probs_full, probs_low, attended_rows = saved
    dim_one, dim_two, feature_count = tokens_in.shape
    inner_width = w_out.shape[0]
    head_count = inner_width // HD
    grad_flat = grad_rows.reshape(-1, feature_count)
    grad_wout = jnp.dot(attended_rows.T, grad_flat, preferred_element_type=jnp.float32)
    d_attended = jnp.dot(grad_flat, w_out.T, preferred_element_type=jnp.float32).astype(jnp.bfloat16)
    d_attended = d_attended.reshape(dim_one, dim_two, head_count, HD)
    d_queries, d_keys, d_values = attend_back(queries, keys_in, values, probs_full, probs_low, d_attended, time_major)
    d_projected = jnp.stack([d_queries, d_keys, d_values], axis=2).reshape(-1, 3 * inner_width)
    grad_wqkv = jnp.dot(normed_low.T, d_projected, preferred_element_type=jnp.float32)
    d_normed = jnp.dot(d_projected, w_qkv.T, preferred_element_type=jnp.float32)
    rows_wide = tokens_in.reshape(-1, feature_count).astype(jnp.float32)
    normed, inverse = normalize(rows_wide)
    d_centre = lax.optimization_barrier(jnp.mean(d_normed, axis=-1, keepdims=True))
    d_spread = lax.optimization_barrier(jnp.mean(d_normed * normed, axis=-1, keepdims=True))
    d_rows = inverse * (d_normed - d_centre - normed * d_spread)
    d_input = (grad_flat.astype(jnp.float32) + d_rows).astype(jnp.bfloat16).reshape(tokens_in.shape)
    return (d_input, grad_wqkv, grad_wout)

def reference(video, w_qkv_space, w_out_space, w_qkv_time, w_out_time, grad_out):

    def one_clip(pair):
        clip_video, clip_grad = pair
        space_out, space_saved = block_forward(clip_video, w_qkv_space, w_out_space, False)
        time_out, time_saved = block_forward(space_out, w_qkv_time, w_out_time, True)
        d_space, g_qkv_time, g_out_time = block_backward(space_out, time_saved, clip_grad, w_qkv_time, w_out_time, True)
        d_video, g_qkv_space, g_out_space = block_backward(clip_video, space_saved, d_space, w_qkv_space, w_out_space, False)
        return (time_out, d_video, g_qkv_space, g_out_space, g_qkv_time, g_out_time)
    per_clip = lax.map(one_clip, (video, grad_out))
    return (per_clip[0], per_clip[1], lax.optimization_barrier(jnp.sum(per_clip[2], axis=0)), lax.optimization_barrier(jnp.sum(per_clip[3], axis=0)), lax.optimization_barrier(jnp.sum(per_clip[4], axis=0)), lax.optimization_barrier(jnp.sum(per_clip[5], axis=0)))
```

```python
import math

import jax
import jax.numpy as jnp
from jax import lax
from jax.experimental import pallas as pl
from jax.experimental.pallas import tpu as pltpu
from jax.sharding import PartitionSpec as P

HD = 64


epsilon = 1e-05


def forms(time_major):
    if time_major:
        return ("lbhd", "mbhd")
    return ("blhd", "bmhd")


def normalize(rows_wide):
    centre_mean = jnp.mean(rows_wide, axis=-1, keepdims=True)
    centred = rows_wide - centre_mean
    variance = jnp.mean(centred * centred, axis=-1, keepdims=True)
    inverse = lax.rsqrt(variance + epsilon)
    return (centred * inverse, inverse)


def attend(queries, keys_in, values, time_major):
    query_form, key_form = forms(time_major)
    factor = 1.0 / math.sqrt(HD)
    scores = (
        jnp.einsum(
            query_form + "," + key_form + "->bhlm",
            queries.astype(jnp.float32),
            keys_in.astype(jnp.float32),
        )
        * factor
    )
    highest = jnp.max(scores, axis=-1, keepdims=True)
    weights = jnp.exp(scores - highest)
    probs_full = weights / jnp.sum(weights, axis=-1, keepdims=True)
    probs_low = lax.optimization_barrier(probs_full.astype(jnp.bfloat16))
    attended = jnp.einsum(
        "bhlm," + key_form + "->" + query_form,
        probs_low.astype(jnp.float32),
        values.astype(jnp.float32),
    )
    return (attended.astype(jnp.bfloat16), probs_full, probs_low)


def attend_back(queries, keys_in, values, probs_full, probs_low, d_attended, time_major):
    query_form, key_form = forms(time_major)
    factor = 1.0 / math.sqrt(HD)
    d_wide = d_attended.astype(jnp.float32)
    d_values = jnp.einsum(
        "bhlm," + query_form + "->" + key_form, probs_low.astype(jnp.float32), d_wide
    )
    d_probs = jnp.einsum(query_form + "," + key_form + "->bhlm", d_wide, values.astype(jnp.float32))
    d_scores = (
        probs_full * (d_probs - jnp.sum(d_probs * probs_full, axis=-1, keepdims=True)) * factor
    )
    d_queries = jnp.einsum(
        "bhlm," + key_form + "->" + query_form, d_scores, keys_in.astype(jnp.float32)
    )
    d_keys = jnp.einsum(
        "bhlm," + query_form + "->" + key_form, d_scores, queries.astype(jnp.float32)
    )
    return (
        d_queries.astype(jnp.bfloat16),
        d_keys.astype(jnp.bfloat16),
        d_values.astype(jnp.bfloat16),
    )


def block_forward(tokens_in, w_qkv, w_out, time_major):
    dim_one, dim_two, feature_count = tokens_in.shape
    head_count = w_out.shape[0] // HD
    rows_wide = tokens_in.reshape(-1, feature_count).astype(jnp.float32)
    normed, _ = normalize(rows_wide)
    normed_low = normed.astype(jnp.bfloat16)
    projected = jnp.dot(normed_low, w_qkv, preferred_element_type=jnp.float32).astype(jnp.bfloat16)
    pieces = projected.reshape(dim_one, dim_two, 3, head_count, HD)
    queries = pieces[:, :, 0]
    keys_in = pieces[:, :, 1]
    values = pieces[:, :, 2]
    attended, probs_full, probs_low = attend(queries, keys_in, values, time_major)
    attended_rows = attended.reshape(-1, w_out.shape[0])
    summed = rows_wide + jnp.dot(attended_rows, w_out, preferred_element_type=jnp.float32)
    output_rows = summed.astype(jnp.bfloat16).reshape(tokens_in.shape)
    return (
        output_rows,
        (normed_low, queries, keys_in, values, probs_full, probs_low, attended_rows),
    )


def block_backward(tokens_in, saved, grad_rows, w_qkv, w_out, time_major):
    normed_low, queries, keys_in, values, probs_full, probs_low, attended_rows = saved
    dim_one, dim_two, feature_count = tokens_in.shape
    inner_width = w_out.shape[0]
    head_count = inner_width // HD
    grad_flat = grad_rows.reshape(-1, feature_count)
    grad_wout = jnp.dot(attended_rows.T, grad_flat, preferred_element_type=jnp.float32)
    d_attended = jnp.dot(grad_flat, w_out.T, preferred_element_type=jnp.float32).astype(
        jnp.bfloat16
    )
    d_attended = d_attended.reshape(dim_one, dim_two, head_count, HD)
    d_queries, d_keys, d_values = attend_back(
        queries, keys_in, values, probs_full, probs_low, d_attended, time_major
    )
    d_projected = jnp.stack([d_queries, d_keys, d_values], axis=2).reshape(-1, 3 * inner_width)
    grad_wqkv = jnp.dot(normed_low.T, d_projected, preferred_element_type=jnp.float32)
    d_normed = jnp.dot(d_projected, w_qkv.T, preferred_element_type=jnp.float32)
    rows_wide = tokens_in.reshape(-1, feature_count).astype(jnp.float32)
    normed, inverse = normalize(rows_wide)
    d_centre = jnp.mean(d_normed, axis=-1, keepdims=True)
    d_spread = jnp.mean(d_normed * normed, axis=-1, keepdims=True)
    d_rows = inverse * (d_normed - d_centre - normed * d_spread)
    d_input = (grad_flat.astype(jnp.float32) + d_rows).astype(jnp.bfloat16).reshape(tokens_in.shape)
    return (d_input, grad_wqkv, grad_wout)


MESH = pl.DeviceIdType.MESH

def coords():
    dp = lax.axis_index("dp"); seq = lax.axis_index("seq")
    return dict(y=dp % 4, z=(dp // 4) * 4 + seq // 8, x=(seq // 2) % 4, c=seq % 2)

def place(x, y, z, c):
    return ((z // 4) * 4 + y, (z % 4) * 8 + x * 2 + c)

def red_kernel(gt, gs, oq0, oo0, oq1, oo1, r1, a, r2, b, r3, cc, r4, d, r5, e, f, ssem, rsem):
    G = (gt, gs)
    me = coords()
    x, y, z, c = me["x"], me["y"], me["z"], me["c"]
    even = (z % 2) == 0
    tie = 1 - 2 * (z % 2)
    xs = [place((x + k) % 4, y, z, c) for k in (1, 2, 3)]
    ys = [place(x, (y + k) % 4, z, c) for k in (1, 2, 3)]
    zoff = [1, 7, (8 + 2 * tie) % 8]
    zt = [place(x, y, (z + o) % 8, c) for o in zoff]
    zs = [place(x, y, (z + 8 - o) % 8, c) for o in zoff]
    zh = place(x, y, (z + 4) % 8, c)
    core = place(x, y, z, 1 - c)
    barrier = pltpu.get_barrier_semaphore()
    for p in xs + ys + zs + [zh, core]:
        pl.semaphore_signal(barrier, inc=1, device_id=p, device_id_type=MESH)
    pl.semaphore_wait(barrier, 11)
    targets = {"x": [(p, (x + k) % 4) for p, k in zip(xs, (1, 2, 3))],
               "y": [(p, (y + k) % 4) for p, k in zip(ys, (1, 2, 3))],
               "z": [(p, (z + o) % 4) for p, o in zip(zt, zoff)]}
    own = {"x": x, "y": y, "z": z % 4}
    orders = ("xyz", "yzx", "zxy")

    def send(src, dst, h, s, dev):
        pltpu.make_async_remote_copy(src, dst, ssem.at[h, s], rsem.at[h, s], device_id=dev, device_id_type=MESH).start()

    def done(ref, sem):
        pltpu.make_async_copy(ref, ref, sem).wait()

    H = (0, 1)
    for h in H:
        send(G[h].at[1 - c], r1.at[h], h, 0, core)
    for h in H:
        done(r1.at[h], rsem.at[h, 0])
        for j in range(3):
            def body(i, _):
                a[h, j, i] = (G[h][c, j, i].astype(jnp.float32) + r1[h, j, i].astype(jnp.float32)).astype(jnp.bfloat16)
                return 0
            lax.fori_loop(0, 4, body, 0)
            for k, (dev, o) in enumerate(targets[orders[j][0]]):
                send(a.at[h, j, o], r2.at[h, j, k], h, 1 + j, dev)
    for h in H:
        for j in range(3):
            done(r2.at[h, j], rsem.at[h, 1 + j])
            o0 = own[orders[j][0]]
            def body(i, _):
                t = a[h, j, o0, i].astype(jnp.float32)
                for k in range(3):
                    t = t + r2[h, j, k, i].astype(jnp.float32)
                b[h, j, i] = t.astype(jnp.bfloat16)
                return 0
            lax.fori_loop(0, 4, body, 0)
            for k, (dev, o) in enumerate(targets[orders[j][1]]):
                send(b.at[h, j, o], r3.at[h, j, k], h, 4 + j, dev)
    for h in H:
        for j in range(3):
            done(r3.at[h, j], rsem.at[h, 4 + j])
            t = b[h, j, own[orders[j][1]]].astype(jnp.float32)
            for k in range(3):
                t = t + r3[h, j, k].astype(jnp.float32)
            cc[h, j] = t.astype(jnp.bfloat16)
            for k, (dev, o) in enumerate(targets[orders[j][2]]):
                send(cc.at[h, j, o], r4.at[h, j, k], h, 7 + j, dev)
    for h in H:
        for j in range(3):
            done(r4.at[h, j], rsem.at[h, 7 + j])
            t = cc[h, j, own[orders[j][2]]].astype(jnp.float32)
            for k in range(3):
                t = t + r4[h, j, k].astype(jnp.float32)
            d[h, j] = t.astype(jnp.bfloat16)
        send(d.at[h], r5.at[h], h, 10, zh)
    for h in H:
        done(r5.at[h], rsem.at[h, 10])
        e[h] = (d[h].astype(jnp.float32) + r5[h].astype(jnp.float32)).astype(jnp.bfloat16)
        for k, dev in enumerate(ys):
            send(e.at[h], f.at[h, k], h, 11, dev)
    outs = ((oq0, oo0), (oq1, oo1))
    for h in H:
        done(f.at[h], rsem.at[h, 11])
        for k in range(4):
            blk = (e[h] if k == 0 else f[h, k - 1]).astype(jnp.float32).reshape(48, 384)
            src = (y + 4 - k) % 4
            for t in range(4):
                @pl.when(src == t)
                def _():
                    if t < 3:
                        outs[h][0][:, 768 * t:768 * t + 384] = blk[:24]
                        outs[h][0][:, 768 * t + 384:768 * t + 768] = blk[24:]
                    else:
                        outs[h][1][:, :384] = blk[:24]
                        outs[h][1][:, 384:] = blk[24:]
    for h in H:
        done(r1.at[h], ssem.at[h, 0])
        for j in range(3):
            done(r2.at[h, j], ssem.at[h, 1 + j])
            done(r3.at[h, j], ssem.at[h, 4 + j])
            done(r4.at[h, j], ssem.at[h, 7 + j])
        done(r5.at[h], ssem.at[h, 10])
        done(f.at[h], ssem.at[h, 11])

def reduce_call(gt, gs):
    bf = jnp.bfloat16
    V = lambda *s: pltpu.VMEM(s, bf)
    vm = pl.BlockSpec(memory_space=pltpu.VMEM)
    return pl.pallas_call(
        red_kernel,
        out_shape=[jax.ShapeDtypeStruct((24, 2304), jnp.float32), jax.ShapeDtypeStruct((24, 768), jnp.float32)] * 2,
        in_specs=[vm] * 2, out_specs=[vm] * 4,
        scratch_shapes=[V(2, 3, 4, 4, 4, 16, 384), V(2, 3, 4, 4, 4, 16, 384), V(2, 3, 3, 4, 4, 16, 384), V(2, 3, 4, 4, 16, 384),
                        V(2, 3, 3, 4, 16, 384), V(2, 3, 4, 16, 384), V(2, 3, 3, 16, 384), V(2, 3, 16, 384), V(2, 3, 16, 384),
                        V(2, 3, 16, 384), V(2, 3, 3, 16, 384),
                        pltpu.SemaphoreType.DMA((2, 12)), pltpu.SemaphoreType.DMA((2, 12))],
        compiler_params=pltpu.CompilerParams(collective_id=0, has_side_effects=True, vmem_limit_bytes=56 * 2**20),
        name="reduce_grads",
    )(gt, gs)

def lay(gq, go):
    g = jnp.concatenate([gq, go], axis=1).astype(jnp.bfloat16)
    g = g.reshape(4, 4, 2, 24, 4, 2, 384)
    g = g.transpose(2, 0, 1, 4, 5, 3, 6).reshape(2, 4, 4, 4, 3, 16, 384)
    g0 = g[:, :, :, :, 0].transpose(0, 2, 3, 1, 4, 5)
    g1 = g[:, :, :, :, 1].transpose(0, 3, 1, 2, 4, 5)
    g2 = g[:, :, :, :, 2]
    return jnp.stack([g0, g1, g2], axis=1)


def shards(video, w_qkv_space, w_out_space, w_qkv_time, w_out_time, grad_out):
    frames_here = video[0]
    group_size = lax.axis_size("seq")
    frames_dev, patch_total, feature_count = frames_here.shape
    patch_share = patch_total // group_size
    space_out, space_saved = block_forward(frames_here, w_qkv_space, w_out_space, False)
    space_parts = space_out.reshape(frames_dev, group_size, patch_share, feature_count)
    grad_parts = grad_out[0].reshape(frames_dev, group_size, patch_share, feature_count)
    arrived = lax.all_to_all(space_parts, "seq", split_axis=1, concat_axis=0, tiled=True)
    time_in = arrived[:, 0]
    time_out, time_saved = block_forward(time_in, w_qkv_time, w_out_time, True)
    returned = lax.all_to_all(time_out[:, None], "seq", split_axis=0, concat_axis=1, tiled=True)
    grad_arrived = lax.all_to_all(grad_parts, "seq", split_axis=1, concat_axis=0, tiled=True)
    d_time_in, g_qkv_time, g_out_time = block_backward(
        time_in, time_saved, grad_arrived[:, 0], w_qkv_time, w_out_time, True
    )
    d_space = lax.all_to_all(d_time_in[:, None], "seq", split_axis=0, concat_axis=1, tiled=True)
    d_space = d_space.reshape(frames_dev, patch_total, feature_count)
    d_video, g_qkv_space, g_out_space = block_backward(
        frames_here, space_saved, d_space, w_qkv_space, w_out_space, False
    )
    reduced = reduce_call(lay(g_qkv_space, g_out_space), lay(g_qkv_time, g_out_time))
    output_frames = returned.reshape(frames_dev, patch_total, feature_count)[None]
    return (output_frames, d_video[None], reduced[0], reduced[1], reduced[2], reduced[3])


def solution(mesh):
    return jax.shard_map(
        shards,
        mesh=mesh,
        in_specs=(P("dp", "seq", None, None), P(), P(), P(), P(), P("dp", "seq", None, None)),
        out_specs=(
            P("dp", "seq", None, None),
            P("dp", "seq", None, None),
            P("seq", None),
            P("seq", None),
            P("seq", None),
            P("seq", None),
        ),
        check_vma=False,
    )
```

```python
import math

import jax
import jax.numpy as jnp
from jax import lax
from jax.experimental import pallas as pl
from jax.experimental.pallas import tpu as pltpu
from jax.sharding import PartitionSpec as P

MESH = pl.DeviceIdType.MESH
F32 = jnp.float32
BF16 = jnp.bfloat16
HD = 64
D = 768
ROWS = 256
PAIRS = 6
GROUP = 32
EPSILON = 1e-05
SCALE = 1.0 / math.sqrt(HD)
SCALE_LOG2E = SCALE * math.log2(math.e)
ORDERS = ("xyz", "yzx", "zxy")
TIME, SPACE = 0, 1


def place(x, y, z, c):
    return ((z // 4) * 4 + y, (z % 4) * 8 + x * 2 + c)


def mm(a, b):
    return jnp.dot(a, b, preferred_element_type=F32)


def mm_nt(a, b):
    return lax.dot_general(a, b, (((1,), (1,)), ((), ())), preferred_element_type=F32)


def mm_tn(a, b):
    return lax.dot_general(a, b, (((0,), (0,)), ((), ())), preferred_element_type=F32)


def normalize(rows):
    mean = jnp.mean(rows, axis=-1, keepdims=True)
    centred = rows - mean
    variance = jnp.mean(centred * centred, axis=-1, keepdims=True)
    inverse = lax.rsqrt(variance + EPSILON)
    return centred * inverse, inverse


def normalize_back(rows, d_normed):
    normed, inverse = normalize(rows)
    d_centre = jnp.mean(d_normed, axis=-1, keepdims=True)
    d_spread = jnp.mean(d_normed * normed, axis=-1, keepdims=True)
    return inverse * (d_normed - d_centre - normed * d_spread)


def pack(rows):
    cut = rows.reshape(GROUP, 8, D)
    return jnp.concatenate([cut[:, :, : D // 2], cut[:, :, D // 2 :]], axis=1).astype(BF16)


def unpack(blocks):
    wide = blocks.astype(F32)
    return jnp.concatenate([wide[:, :8], wide[:, 8:]], axis=2).reshape(ROWS, D)


def softmax(scores):
    highest = jnp.max(scores, axis=-1, keepdims=True)
    weights = jnp.exp2((scores - highest) * SCALE_LOG2E)
    return weights * (1.0 / jnp.sum(weights, axis=-1, keepdims=True))


def kernel(
    video, wqs, wos, wqt, wot, gout,
    out_video, grad_video, oqs, oos, oqt, oot,
    vid_v, gout_v, wqs_v, wos_v, wqt_v, wot_v,
    qkv_s, qkv_t, att_s, att_t, dqkv, datt, tin, gt, nT, aT, nTs, aTs,
    probs_s, probs_t, perm, permT, outv, gradv,
    sbuf, rbuf, G, r1, r2, b, r3, cc, r4, d, r5, e, f,
    lsem, asem, arsem, ssem, rsem,
):
    dp, seq = lax.axis_index("dp"), lax.axis_index("seq")
    x, y, z, c = (seq // 2) % 4, dp % 4, (dp // 4) * 4 + seq // 8, seq % 2
    tie = 1 - 2 * (z % 2)
    xs = [place((x + k) % 4, y, z, c) for k in (1, 2, 3)]
    ys = [place(x, (y + k) % 4, z, c) for k in (1, 2, 3)]
    zoff = [1, 7, (8 + 2 * tie) % 8]
    zt = [place(x, y, (z + o) % 8, c) for o in zoff]
    zs = [place(x, y, (z + 8 - o) % 8, c) for o in zoff]
    zh = place(x, y, (z + 4) % 8, c)
    core = place(x, y, z, 1 - c)
    targets = {
        "x": [(p, (x + k) % 4) for p, k in zip(xs, (1, 2, 3))],
        "y": [(p, (y + k) % 4) for p, k in zip(ys, (1, 2, 3))],
        "z": [(p, (z + o) % 4) for p, o in zip(zt, zoff)],
    }
    own = {"x": x, "y": y, "z": z % 4}

    loads = [
        pltpu.make_async_copy(src, dst, lsem.at[i])
        for i, (src, dst) in enumerate(
            ((video, vid_v), (wqs, wqs_v), (wos, wos_v), (gout, gout_v), (wqt, wqt_v), (wot, wot_v))
        )
    ]
    for load in loads:
        load.start()

    barrier = pltpu.get_barrier_semaphore()

    def greet(k, _):
        pl.semaphore_signal(barrier, inc=1, device_id=(dp, (seq + k) % GROUP), device_id_type=MESH)
        return 0

    lax.fori_loop(1, GROUP, greet, 0)
    for peer in ys + zs + [zh]:
        pl.semaphore_signal(barrier, inc=1, device_id=peer, device_id_type=MESH)

    def done(ref, sem):
        pltpu.make_async_copy(ref, ref, sem).wait()

    def exchange(i):
        def one(k, _):
            to = (seq + k) % GROUP
            pltpu.make_async_remote_copy(
                sbuf.at[i, to], rbuf.at[i, seq], asem.at[i], arsem.at[i],
                device_id=(dp, to), device_id_type=MESH,
            ).start()
            return 0

        lax.fori_loop(1, GROUP, one, 0)
        rbuf[i, seq] = sbuf[i, seq]

    def arrived(i):
        done(rbuf.at[i, pl.ds(0, GROUP - 1)], arsem.at[i])

    def send(src, dst, h, s, dev):
        pltpu.make_async_remote_copy(
            src, dst, ssem.at[h, s], rsem.at[h, s], device_id=dev, device_id_type=MESH
        ).start()

    def sum_core_start(h):
        send(G.at[h, 1 - c], r1.at[h], h, 0, core)

    def sum_first(h):
        done(r1.at[h], rsem.at[h, 0])
        for j in range(3):
            def body(i, _):
                r1[h, j, i] = (G[h, c, j, i].astype(F32) + r1[h, j, i].astype(F32)).astype(BF16)
                return 0

            lax.fori_loop(0, 4, body, 0)
            for k, (dev, o) in enumerate(targets[ORDERS[j][0]]):
                send(r1.at[h, j, o], r2.at[h, j, k], h, 1 + j, dev)

    def sum_second(h):
        for j in range(3):
            done(r2.at[h, j], rsem.at[h, 1 + j])
            o0 = own[ORDERS[j][0]]

            def body(i, _):
                t = r1[h, j, o0, i].astype(F32)
                for k in range(3):
                    t = t + r2[h, j, k, i].astype(F32)
                b[h, j, i] = t.astype(BF16)
                return 0

            lax.fori_loop(0, 4, body, 0)
            for k, (dev, o) in enumerate(targets[ORDERS[j][1]]):
                send(b.at[h, j, o], r3.at[h, j, k], h, 4 + j, dev)

    def sum_third(h):
        for j in range(3):
            done(r3.at[h, j], rsem.at[h, 4 + j])
            t = b[h, j, own[ORDERS[j][1]]].astype(F32)
            for k in range(3):
                t = t + r3[h, j, k].astype(F32)
            cc[h, j] = t.astype(BF16)
            for k, (dev, o) in enumerate(targets[ORDERS[j][2]]):
                send(cc.at[h, j, o], r4.at[h, j, k], h, 7 + j, dev)

    def sum_far(h):
        for j in range(3):
            done(r4.at[h, j], rsem.at[h, 7 + j])
            t = cc[h, j, own[ORDERS[j][2]]].astype(F32)
            for k in range(3):
                t = t + r4[h, j, k].astype(F32)
            d[h, j] = t.astype(BF16)
        send(d.at[h], r5.at[h], h, 10, zh)

    def sum_gather(h):
        done(r5.at[h], rsem.at[h, 10])
        e[h] = (d[h].astype(F32) + r5[h].astype(F32)).astype(BF16)
        for k, dev in enumerate(ys):
            send(e.at[h], f.at[h, k], h, 11, dev)

    def sum_finish(h, wide_out, narrow_out):
        done(f.at[h], rsem.at[h, 11])
        for k in range(4):
            block = (e[h] if k == 0 else f[h, k - 1]).astype(F32).reshape(48, D // 2)
            source = (y + 4 - k) % 4
            for t in range(4):
                @pl.when(source == t)
                def _():
                    out, at = (wide_out, D * t) if t < 3 else (narrow_out, 0)
                    out[:, at : at + D // 2] = block[:24]
                    out[:, at + D // 2 : at + D] = block[24:]

    def sum_sent(h):
        done(r1.at[h], ssem.at[h, 0])
        for j in range(3):
            done(r2.at[h, j], ssem.at[h, 1 + j])
            done(r3.at[h, j], ssem.at[h, 4 + j])
            done(r4.at[h, j], ssem.at[h, 7 + j])
        done(r5.at[h], ssem.at[h, 10])
        done(f.at[h], ssem.at[h, 11])

    def write_grad(h, left, right, part):
        def body(zp, _):
            block = mm(left[pl.ds(pl.multiple_of(192 * zp, 16), 192), :], right)
            for i in range(8):
                xp, cp = i // 2, i % 2
                own_rows = block[24 * i : 24 * i + 24]
                own_rows = jnp.concatenate([own_rows[:, : D // 2], own_rows[:, D // 2 :]], axis=0).astype(BF16)
                G[h, cp, 0, xp, part, zp] = own_rows[0:16]
                G[h, cp, 1, part, zp, xp] = own_rows[16:32]
                G[h, cp, 2, zp, xp, part] = own_rows[32:48]
            return 0

        lax.fori_loop(0, 4, body, 0)

    left_half = lax.broadcasted_iota(jnp.int32, (1, 128), 1) < HD

    def halves(value):
        zero = jnp.zeros_like(value)
        return jnp.where(left_half, value, zero), jnp.where(left_half, zero, value)

    def columns(pair, part):
        return pl.ds(pl.multiple_of(part * D + pair * 128, 128), 128)

    def attend(qkv, probs, att, size, mask):
        def body(pair, _):
            for blk in range(ROWS // size):
                rows = slice(blk * size, blk * size + size)
                queries = halves(qkv[rows, columns(pair, 0)])
                keys = qkv[rows, columns(pair, 1)]
                values = halves(qkv[rows, columns(pair, 2)])
                total = None
                for s in range(2):
                    scores = mm_nt(queries[s], keys)
                    if mask is not None:
                        scores = jnp.where(mask, scores, -1e30)
                    low = softmax(scores).astype(BF16)
                    probs[pair * 2 + s, rows] = low
                    part = mm(low, values[s])
                    total = part if total is None else total + part
                att[rows, columns(pair, 0)] = total.astype(BF16)
            return 0

        lax.fori_loop(0, PAIRS, body, 0)

    def attend_back(qkv, probs, size, first, last):
        def body(pair, _):
            for blk in range(ROWS // size):
                rows = slice(blk * size, blk * size + size)
                queries = halves(qkv[rows, columns(pair, 0)])
                keys = halves(qkv[rows, columns(pair, 1)])
                values = qkv[rows, columns(pair, 2)]
                d_out = halves(datt[rows, columns(pair, 0)])
                d_queries = d_keys = d_values = 0.0
                for s in range(2):
                    low = probs[pair * 2 + s, rows]
                    wide = low.astype(F32)
                    d_probs = mm_nt(d_out[s], values)
                    product = d_probs * wide
                    d_scores = (product - wide * jnp.sum(product, axis=-1, keepdims=True)).astype(BF16)
                    d_values = d_values + mm_tn(low, d_out[s])
                    d_queries = d_queries + mm(d_scores, keys[s])
                    d_keys = d_keys + mm_tn(d_scores, queries[s])
                dqkv[rows, columns(pair, 0)] = (d_queries * SCALE).astype(BF16)
                dqkv[rows, columns(pair, 1)] = (d_keys * SCALE).astype(BF16)
                dqkv[rows, columns(pair, 2)] = d_values.astype(BF16)
            return 0

        lax.fori_loop(first, last, body, 0)

    def project(normed, weights, qkv):
        for part in range(3):
            at = slice(part * D, part * D + D)
            qkv[:, at] = mm(normed, weights[:, at]).astype(BF16)

    def project_back(weights):
        total = mm_nt(dqkv[:, :D], weights[:, :D])
        for part in (1, 2):
            at = slice(part * D, part * D + D)
            total = total + mm_nt(dqkv[:, at], weights[:, at])
        return total

    loads[0].wait()
    rows_in = vid_v[...].astype(F32)
    normed = normalize(rows_in)[0].astype(BF16)
    loads[1].wait()
    project(normed, wqs_v, qkv_s)
    nTs[...] = normed.T
    loads[3].wait()
    sbuf[0] = pack(gout_v[...].astype(F32))
    pl.semaphore_wait(barrier, GROUP - 1 + 7)
    exchange(0)
    attend(qkv_s, probs_s, att_s, ROWS, None)
    loads[2].wait()
    sbuf[1] = pack(vid_v[...].astype(F32) + mm(att_s[...], wos_v[...]))
    exchange(1)

    r = lax.broadcasted_iota(jnp.int32, (ROWS, ROWS), 0)
    q = lax.broadcasted_iota(jnp.int32, (ROWS, ROWS), 1)
    perm[...] = jnp.where(q == (r % 32) * 8 + r // 32, 1.0, 0.0).astype(BF16)
    permT[...] = jnp.where(r == (q % 32) * 8 + q // 32, 1.0, 0.0).astype(BF16)
    aTs[...] = att_s[...].T
    arrived(0)
    gt[...] = mm(perm[...], unpack(rbuf[0]).astype(BF16)).astype(BF16)
    loads[4].wait()
    loads[5].wait()
    datt[...] = mm_nt(gt[...], wot_v[...]).astype(BF16)
    arrived(1)

    rows_in = mm(perm[...], unpack(rbuf[1]).astype(BF16))
    tin[...] = rows_in.astype(BF16)
    normed = normalize(rows_in)[0].astype(BF16)
    project(normed, wqt_v, qkv_t)
    nT[...] = normed.T
    same = (
        lax.broadcasted_iota(jnp.int32, (128, 128), 0) // 32
        == lax.broadcasted_iota(jnp.int32, (128, 128), 1) // 32
    )
    attend(qkv_t, probs_t, att_t, 128, same)
    low = (tin[...].astype(F32) + mm(att_t[...], wot_v[...])).astype(BF16)
    sbuf[2] = pack(mm(permT[...], low))
    exchange(2)
    attend_back(qkv_t, probs_t, 128, 0, PAIRS)
    d_rows = normalize_back(tin[...].astype(F32), project_back(wqt_v))
    low = (gt[...].astype(F32) + d_rows).astype(BF16)
    sbuf[3] = pack(mm(permT[...], low))
    exchange(3)
    aT[...] = att_t[...].T
    for part in range(3):
        write_grad(TIME, nT, dqkv[:, part * D : part * D + D], part)
    write_grad(TIME, aT, gt[...], 3)
    sum_core_start(TIME)
    arrived(2)
    outv[...] = unpack(rbuf[2]).astype(BF16)
    out_copy = pltpu.make_async_copy(outv, out_video, lsem.at[6])
    out_copy.start()
    arrived(3)

    d_space = unpack(rbuf[3]).astype(BF16)
    datt[...] = mm_nt(d_space, wos_v[...]).astype(BF16)
    write_grad(SPACE, aTs, d_space, 3)
    attend_back(qkv_s, probs_s, ROWS, 0, 2)
    sum_first(TIME)
    attend_back(qkv_s, probs_s, ROWS, 2, 4)
    sum_second(TIME)
    attend_back(qkv_s, probs_s, ROWS, 4, 6)
    sum_third(TIME)
    for part in range(3):
        write_grad(SPACE, nTs, dqkv[:, part * D : part * D + D], part)
    sum_core_start(SPACE)
    sum_far(TIME)
    d_rows = normalize_back(vid_v[...].astype(F32), project_back(wqs_v))
    gradv[...] = (unpack(rbuf[3]) + d_rows).astype(BF16)
    grad_copy = pltpu.make_async_copy(gradv, grad_video, lsem.at[7])
    grad_copy.start()
    sum_gather(TIME)
    sum_first(SPACE)
    sum_finish(TIME, oqt, oot)
    sum_second(SPACE)
    sum_third(SPACE)
    sum_far(SPACE)
    sum_gather(SPACE)
    sum_finish(SPACE, oqs, oos)
    for i in range(4):
        done(rbuf.at[i, pl.ds(0, GROUP - 1)], asem.at[i])
    sum_sent(TIME)
    sum_sent(SPACE)
    out_copy.wait()
    grad_copy.wait()


def shards(video, w_qkv_space, w_out_space, w_qkv_time, w_out_time, grad_out):
    V = lambda *s: pltpu.VMEM(s, BF16)
    anywhere = pl.BlockSpec(memory_space=pl.ANY)
    vmem = pl.BlockSpec(memory_space=pltpu.VMEM)
    tokens = jax.ShapeDtypeStruct((ROWS, D), BF16)
    wide = jax.ShapeDtypeStruct((24, 3 * D), F32)
    narrow = jax.ShapeDtypeStruct((24, D), F32)
    outs = pl.pallas_call(
        kernel,
        out_shape=[tokens, tokens, wide, narrow, wide, narrow],
        in_specs=[anywhere] * 6,
        out_specs=[anywhere] * 2 + [vmem] * 4,
        scratch_shapes=[
            V(ROWS, D), V(ROWS, D), V(D, 3 * D), V(D, D), V(D, 3 * D), V(D, D),
            V(ROWS, 3 * D), V(ROWS, 3 * D), V(ROWS, D), V(ROWS, D), V(ROWS, 3 * D), V(ROWS, D),
            V(ROWS, D), V(ROWS, D), V(D, ROWS), V(D, ROWS), V(D, ROWS), V(D, ROWS),
            V(12, ROWS, ROWS), V(12, ROWS, 128), V(ROWS, ROWS), V(ROWS, ROWS), V(ROWS, D), V(ROWS, D),
            V(4, GROUP, 16, 384), V(4, GROUP, 16, 384),
            V(2, 2, 3, 4, 4, 4, 16, 384), V(2, 3, 4, 4, 4, 16, 384), V(2, 3, 3, 4, 4, 16, 384),
            V(2, 3, 4, 4, 16, 384), V(2, 3, 3, 4, 16, 384), V(2, 3, 4, 16, 384), V(2, 3, 3, 16, 384),
            V(2, 3, 16, 384), V(2, 3, 16, 384), V(2, 3, 16, 384), V(2, 3, 3, 16, 384),
            pltpu.SemaphoreType.DMA((8,)), pltpu.SemaphoreType.DMA((4,)), pltpu.SemaphoreType.DMA((4,)),
            pltpu.SemaphoreType.DMA((2, 12)), pltpu.SemaphoreType.DMA((2, 12)),
        ],
        compiler_params=pltpu.CompilerParams(
            collective_id=0, has_side_effects=True, vmem_limit_bytes=60 * 2**20
        ),
        name="layer",
    )(
        video.reshape(ROWS, D), w_qkv_space, w_out_space, w_qkv_time, w_out_time, grad_out.reshape(ROWS, D)
    )
    shape = (1, 1, ROWS, D)
    return (outs[0].reshape(shape), outs[1].reshape(shape), outs[2], outs[3], outs[4], outs[5])


def solution(mesh):
    return jax.shard_map(
        shards,
        mesh=mesh,
        in_specs=(P("dp", "seq", None, None), P(), P(), P(), P(), P("dp", "seq", None, None)),
        out_specs=(
            P("dp", "seq", None, None),
            P("dp", "seq", None, None),
            P("seq", None),
            P("seq", None),
            P("seq", None),
            P("seq", None),
        ),
        check_vma=False,
    )
```

```python
import itertools
import math

import jax
import jax.numpy as jnp
from jax import lax
from jax.experimental import pallas as pl
from jax.experimental.pallas import tpu as pltpu
from jax.sharding import PartitionSpec as P

MESH = pl.DeviceIdType.MESH
F32 = jnp.float32
BF16 = jnp.bfloat16
HD = 64
D = 768
HALF = 384
ROWS = 256
PAIRS = 6
GROUP = 32
EPSILON = 1e-05
SCALE = 1.0 / math.sqrt(HD)
SCALE_LOG2E = SCALE * math.log2(math.e)
TIME, SPACE = 0, 1
ORDERS = (
    (("xyz", "yzx", "xzy"), ("xyz", "yzx", "yxz")),
    (("xyz", "yzx", "zxy"), ("xyz", "yzx", "zxy")),
)


def place(x, y, z, c):
    return ((z // 4) * 4 + y, (z % 4) * 8 + x * 2 + c)


def mm(a, b):
    return jnp.dot(a, b, preferred_element_type=F32)


def mm_nt(a, b):
    return lax.dot_general(a, b, (((1,), (1,)), ((), ())), preferred_element_type=F32)


def mm_tn(a, b):
    return lax.dot_general(a, b, (((0,), (0,)), ((), ())), preferred_element_type=F32)


def normalize(rows):
    mean = jnp.mean(rows, axis=-1, keepdims=True)
    centred = rows - mean
    variance = jnp.mean(centred * centred, axis=-1, keepdims=True)
    inverse = lax.rsqrt(variance + EPSILON)
    return centred * inverse, inverse


def normalize_back(rows, d_normed):
    normed, inverse = normalize(rows)
    d_centre = jnp.mean(d_normed, axis=-1, keepdims=True)
    d_spread = jnp.mean(d_normed * normed, axis=-1, keepdims=True)
    return inverse * (d_normed - d_centre - normed * d_spread)


def pack(rows):
    cut = rows.reshape(GROUP, 8, D)
    return jnp.concatenate([cut[:, :, : D // 2], cut[:, :, D // 2 :]], axis=1).astype(BF16)


def unpack(blocks):
    wide = blocks.astype(F32)
    return jnp.concatenate([wide[:, :8], wide[:, 8:]], axis=2).reshape(ROWS, D)


def softmax(scores):
    highest = jnp.max(scores, axis=-1, keepdims=True)
    weights = jnp.exp2((scores - highest) * SCALE_LOG2E)
    return weights * (1.0 / jnp.sum(weights, axis=-1, keepdims=True))


def kernel(
    video, wqs, wos, wqt, wot, gout,
    out_video, grad_video, oqs, oos, oqt, oot,
    vid_v, gout_v, wqs_v, wos_v, wqt_v, wot_v,
    qkv_s, qkv_t, att_s, att_t, dqkv, datt, tin, gt, nT, aT, nTs, aTs,
    probs_s, probs_t, perm, permT, outv, gradv, d_space,
    sbuf, rbuf, G, r1, r2, b, r3, cc, r4, d, r5, e, f,
    lsem, asem, arsem, ssem, rsem,
):
    dp, seq = lax.axis_index("dp"), lax.axis_index("seq")
    x, y, z, c = (seq // 2) % 4, dp % 4, (dp // 4) * 4 + seq // 8, seq % 2
    tie = 1 - 2 * (z % 2)
    xs = [place((x + k) % 4, y, z, c) for k in (1, 2, 3)]
    ys = [place(x, (y + k) % 4, z, c) for k in (1, 2, 3)]
    zoff = [1, 7, (8 + 2 * tie) % 8]
    zt = [place(x, y, (z + o) % 8, c) for o in zoff]
    zs = [place(x, y, (z + 8 - o) % 8, c) for o in zoff]
    zh = place(x, y, (z + 4) % 8, c)
    core = place(x, y, z, 1 - c)
    targets = {
        "x": [(p, (x + k) % 4) for p, k in zip(xs, (1, 2, 3))],
        "y": [(p, (y + k) % 4) for p, k in zip(ys, (1, 2, 3))],
        "z": [(p, (z + o) % 4) for p, o in zip(zt, zoff)],
    }
    own = {"x": x, "y": y, "z": z % 4}

    loads = [
        pltpu.make_async_copy(src, dst, lsem.at[i])
        for i, (src, dst) in enumerate(
            ((video, vid_v), (wqs, wqs_v), (wos, wos_v), (gout, gout_v), (wqt, wqt_v), (wot, wot_v))
        )
    ]
    for i in (0, 3, 1, 2):
        loads[i].start()

    barrier = pltpu.get_barrier_semaphore()

    def greet(k, _):
        pl.semaphore_signal(barrier, inc=1, device_id=(dp, (seq + k) % GROUP), device_id_type=MESH)
        return 0

    lax.fori_loop(1, GROUP, greet, 0)
    for peer in ys + zs + [zh]:
        pl.semaphore_signal(barrier, inc=1, device_id=peer, device_id_type=MESH)

    def done(ref, sem):
        pltpu.make_async_copy(ref, ref, sem).wait()

    def exchange(i, first=1, last=GROUP):
        def one(k, _):
            far = GROUP - k
            to = ((seq // 8 + far // 8) % 4) * 8 + (x + far // 2) % 4 * 2 + (c + far) % 2
            pltpu.make_async_remote_copy(
                sbuf.at[i, to], rbuf.at[i, seq], asem.at[i], arsem.at[i],
                device_id=(dp, to), device_id_type=MESH,
            ).start()
            return 0

        lax.fori_loop(first, last, one, 0)
        if first == 1:
            rbuf[i, seq] = sbuf[i, seq]

    def arrived(i):
        done(rbuf.at[i, pl.ds(0, GROUP - 1)], arsem.at[i])

    def send(src, dst, h, t, s, dev):
        pltpu.make_async_remote_copy(
            src, dst, ssem.at[h, t, s], rsem.at[h, t, s], device_id=dev, device_id_type=MESH
        ).start()

    def sum_core_start(h, t):
        send(G.at[h, t, 1 - c], r1.at[h, t], h, t, 0, core)

    def sum_add(h, t):
        done(r1.at[h, t], rsem.at[h, t, 0])
        for j in range(3):
            def body(i, _):
                r1[h, t, j, i] = (G[h, t, c, j, i].astype(F32) + r1[h, t, j, i].astype(F32)).astype(BF16)
                return 0

            lax.fori_loop(0, 4, body, 0, unroll=True)

    def sum_first(h, t, thirds=(0, 1, 2)):
        for j in thirds:
            for k, (dev, o) in enumerate(targets[ORDERS[h][t][j][0]]):
                send(r1.at[h, t, j, o], r2.at[h, t, j, k], h, t, 1 + j, dev)

    def sum_second(h, t):
        for j in range(3):
            done(r2.at[h, t, j], rsem.at[h, t, 1 + j])
            o0 = own[ORDERS[h][t][j][0]]

            def body(i, _):
                total = r1[h, t, j, o0, i].astype(F32)
                for k in range(3):
                    total = total + r2[h, t, j, k, i].astype(F32)
                b[h, t, j, i] = total.astype(BF16)
                return 0

            lax.fori_loop(0, 4, body, 0, unroll=True)
            for k, (dev, o) in enumerate(targets[ORDERS[h][t][j][1]]):
                send(b.at[h, t, j, o], r3.at[h, t, j, k], h, t, 4 + j, dev)

    def sum_third(h, t):
        for j in range(3):
            done(r3.at[h, t, j], rsem.at[h, t, 4 + j])
            total = b[h, t, j, own[ORDERS[h][t][j][1]]].astype(F32)
            for k in range(3):
                total = total + r3[h, t, j, k].astype(F32)
            for o in range(4):
                piece = total[o // 2, 24 * (o % 2) : 24 * (o % 2) + 24]
                piece = jnp.concatenate([piece, jnp.zeros((8, 128), F32)], axis=0)
                cc[h, t, j, o] = piece.astype(BF16)
            for k, (dev, o) in enumerate(targets[ORDERS[h][t][j][2]]):
                send(cc.at[h, t, j, o], r4.at[h, t, j, k], h, t, 7 + j, dev)

    def sum_far(h, t):
        for j in range(3):
            done(r4.at[h, t, j], rsem.at[h, t, 7 + j])
            total = cc[h, t, j, own[ORDERS[h][t][j][2]]].astype(F32)
            for k in range(3):
                total = total + r4[h, t, j, k].astype(F32)
            d[h, t, j] = total.astype(BF16)
        send(d.at[h, t], r5.at[h, t], h, t, 10, zh)

    def sum_gather(h, t):
        done(r5.at[h, t], rsem.at[h, t, 10])
        e[h, t] = (d[h, t].astype(F32) + r5[h, t].astype(F32)).astype(BF16)
        for k, dev in enumerate(ys):
            send(e.at[h, t], f.at[h, t, k], h, t, 11, dev)

    def sum_finish(h, t, wide_out, narrow_out):
        done(f.at[h, t], rsem.at[h, t, 11])
        for k in range(4):
            block = (e[h, t] if k == 0 else f[h, t, k - 1]).astype(F32)
            source = (y + 4 - k) % 4
            for part in range(4):
                @pl.when(source == part)
                def _():
                    out, at = (wide_out, D * part) if part < 3 else (narrow_out, 0)
                    for j in range(3):
                        start = at + HALF * t + 128 * j
                        out[:, start : start + 128] = block[j, :24]

    def sum_sent(h, t):
        done(r1.at[h, t], ssem.at[h, t, 0])
        for j in range(3):
            done(r2.at[h, t, j], ssem.at[h, t, 1 + j])
            done(r3.at[h, t, j], ssem.at[h, t, 4 + j])
            done(r4.at[h, t, j], ssem.at[h, t, 7 + j])
        done(r5.at[h, t], ssem.at[h, t, 10])
        done(f.at[h, t], ssem.at[h, t, 11])

    def write_grad(h, t, left, left_out, d_out):
        right = jnp.concatenate([dqkv[:, D * part + HALF * t : D * part + HALF * t + HALF] for part in range(3)], axis=1)
        right_out = d_out[:, HALF * t : HALF * t + HALF]

        def body(zp, _):
            rows = pl.ds(pl.multiple_of(384 * zp, 128), 384)
            three = mm(left[rows, :], right)
            parts = [three[:, HALF * part : HALF * part + HALF] for part in range(3)] + [mm(left_out[rows, :], right_out)]

            def piece(part, z2, xp, cp, j):
                start = z2 * 192 + (xp * 2 + cp) * 24
                return parts[part][start : start + 24, 128 * j : 128 * j + 128]

            for j, order in enumerate(ORDERS[h][t]):
                last = order[2]
                spans = {"x": 4, "y": 4, "z": 2}
                spans[last] //= 2
                for xi, yi, zi, cp in itertools.product(*(range(spans[axis]) for axis in "xyz"), range(2)):
                    pair = []
                    for odd in range(2):
                        xp, part, z2 = xi, yi, zi
                        if last == "x":
                            xp = 2 * xi + odd
                        elif last == "y":
                            part = 2 * yi + odd
                        else:
                            z2 = odd
                        pair.append(piece(part, z2, xp, cp, j))
                    at = {"x": xi, "y": yi, "z": zp if last == "z" else 2 * zp + zi}
                    G[h, t, cp, j, at[order[0]], at[order[1]], at[last]] = jnp.concatenate(pair, axis=0).astype(BF16)
            return 0

        lax.fori_loop(0, 2, body, 0)

    left_half = lax.broadcasted_iota(jnp.int32, (1, 128), 1) < HD

    def halves(value):
        zero = jnp.zeros_like(value)
        return jnp.where(left_half, value, zero), jnp.where(left_half, zero, value)

    def columns(pair, part):
        return pl.ds(pl.multiple_of(part * D + pair * 128, 128), 128)

    def attend(qkv, probs, att, size, mask):
        def body(pair, _):
            for blk in range(ROWS // size):
                rows = slice(blk * size, blk * size + size)
                queries = halves(qkv[rows, columns(pair, 0)])
                keys = qkv[rows, columns(pair, 1)]
                values = halves(qkv[rows, columns(pair, 2)])
                total = None
                for s in range(2):
                    scores = mm_nt(queries[s], keys)
                    if mask is not None:
                        scores = jnp.where(mask, scores, -1e30)
                    low = softmax(scores).astype(BF16)
                    probs[pair * 2 + s, rows] = low
                    part = mm(low, values[s])
                    total = part if total is None else total + part
                att[rows, columns(pair, 0)] = total.astype(BF16)
            return 0

        lax.fori_loop(0, PAIRS, body, 0, unroll=True)

    def attend_back(qkv, probs, size, first, last):
        def body(pair, _):
            for blk in range(ROWS // size):
                rows = slice(blk * size, blk * size + size)
                queries = halves(qkv[rows, columns(pair, 0)])
                keys = halves(qkv[rows, columns(pair, 1)])
                values = qkv[rows, columns(pair, 2)]
                d_out = halves(datt[rows, columns(pair, 0)])
                d_queries = d_keys = d_values = 0.0
                for s in range(2):
                    low = probs[pair * 2 + s, rows]
                    wide = low.astype(F32)
                    d_probs = mm_nt(d_out[s], values)
                    product = d_probs * wide
                    d_scores = (product - wide * jnp.sum(product, axis=-1, keepdims=True)).astype(BF16)
                    d_values = d_values + mm_tn(low, d_out[s])
                    d_queries = d_queries + mm(d_scores, keys[s])
                    d_keys = d_keys + mm_tn(d_scores, queries[s])
                dqkv[rows, columns(pair, 0)] = (d_queries * SCALE).astype(BF16)
                dqkv[rows, columns(pair, 1)] = (d_keys * SCALE).astype(BF16)
                dqkv[rows, columns(pair, 2)] = d_values.astype(BF16)
            return 0

        lax.fori_loop(first, last, body, 0, unroll=True)

    def project(normed, weights, qkv):
        for part in range(3):
            at = slice(part * D, part * D + D)
            qkv[:, at] = mm(normed, weights[:, at]).astype(BF16)

    def project_back(weights):
        total = mm_nt(dqkv[:, :D], weights[:, :D])
        for part in (1, 2):
            at = slice(part * D, part * D + D)
            total = total + mm_nt(dqkv[:, at], weights[:, at])
        return total

    loads[0].wait()
    rows_in = vid_v[...].astype(F32)
    normed = normalize(rows_in)[0].astype(BF16)
    loads[3].wait()
    sbuf[0] = pack(gout_v[...].astype(F32))
    pl.semaphore_wait(barrier, GROUP - 1 + 7)
    exchange(0, 1, 20)
    loads[1].wait()
    loads[4].start()
    loads[5].start()
    project(normed, wqs_v, qkv_s)
    nTs[...] = normed.T
    attend(qkv_s, probs_s, att_s, ROWS, None)
    loads[2].wait()
    sbuf[1] = pack(vid_v[...].astype(F32) + mm(att_s[...], wos_v[...]))
    exchange(1)
    exchange(0, 20, GROUP)

    r = lax.broadcasted_iota(jnp.int32, (ROWS, ROWS), 0)
    q = lax.broadcasted_iota(jnp.int32, (ROWS, ROWS), 1)
    perm[...] = jnp.where(q == (r % 32) * 8 + r // 32, 1.0, 0.0).astype(BF16)
    permT[...] = jnp.where(r == (q % 32) * 8 + q // 32, 1.0, 0.0).astype(BF16)
    aTs[...] = att_s[...].T
    arrived(0)
    gt[...] = mm(perm[...], unpack(rbuf[0]).astype(BF16)).astype(BF16)
    loads[4].wait()
    loads[5].wait()
    datt[...] = mm_nt(gt[...], wot_v[...]).astype(BF16)
    arrived(1)

    rows_in = mm(perm[...], unpack(rbuf[1]).astype(BF16))
    tin[...] = rows_in.astype(BF16)
    normed = normalize(rows_in)[0].astype(BF16)
    project(normed, wqt_v, qkv_t)
    nT[...] = normed.T
    same = (
        lax.broadcasted_iota(jnp.int32, (128, 128), 0) // 32
        == lax.broadcasted_iota(jnp.int32, (128, 128), 1) // 32
    )
    attend(qkv_t, probs_t, att_t, 128, same)
    attend_back(qkv_t, probs_t, 128, 0, PAIRS)
    d_rows = normalize_back(tin[...].astype(F32), project_back(wqt_v))
    low = (gt[...].astype(F32) + d_rows).astype(BF16)
    sbuf[3] = pack(mm(permT[...], low))
    exchange(3)
    aT[...] = att_t[...].T
    for t in range(2):
        write_grad(TIME, t, nT, aT, gt)
        sum_core_start(TIME, t)
    low = (tin[...].astype(F32) + mm(att_t[...], wot_v[...])).astype(BF16)
    sbuf[2] = pack(mm(permT[...], low))
    for t in range(2):
        sum_add(TIME, t)
        sum_first(TIME, t)
    arrived(3)
    exchange(2)

    d_space[...] = unpack(rbuf[3]).astype(BF16)
    datt[...] = mm_nt(d_space[...], wos_v[...]).astype(BF16)
    attend_back(qkv_s, probs_s, ROWS, 0, 3)
    write_grad(SPACE, 0, nTs, aTs, d_space)
    sum_core_start(SPACE, 0)
    attend_back(qkv_s, probs_s, ROWS, 3, 6)
    sum_add(SPACE, 0)
    sum_first(SPACE, 0)
    write_grad(SPACE, 1, nTs, aTs, d_space)
    sum_core_start(SPACE, 1)
    d_rows = normalize_back(vid_v[...].astype(F32), project_back(wqs_v))
    gradv[...] = (d_space[...].astype(F32) + d_rows).astype(BF16)
    grad_copy = pltpu.make_async_copy(gradv, grad_video, lsem.at[7])
    grad_copy.start()
    sum_add(SPACE, 1)
    sum_first(SPACE, 1)
    sum_second(TIME, 0)
    sum_second(TIME, 1)
    arrived(2)
    outv[...] = unpack(rbuf[2]).astype(BF16)
    out_copy = pltpu.make_async_copy(outv, out_video, lsem.at[6])
    out_copy.start()
    sum_second(SPACE, 0)
    sum_third(TIME, 0)
    sum_third(TIME, 1)
    sum_second(SPACE, 1)
    sum_third(SPACE, 0)
    sum_far(TIME, 0)
    sum_far(TIME, 1)
    sum_third(SPACE, 1)
    sum_far(SPACE, 0)
    sum_gather(TIME, 0)
    sum_gather(TIME, 1)
    sum_far(SPACE, 1)
    sum_gather(SPACE, 0)
    sum_finish(TIME, 0, oqt, oot)
    sum_finish(TIME, 1, oqt, oot)
    sum_gather(SPACE, 1)
    sum_finish(SPACE, 0, oqs, oos)
    sum_finish(SPACE, 1, oqs, oos)
    for i in range(4):
        done(rbuf.at[i, pl.ds(0, GROUP - 1)], asem.at[i])
    for t in range(2):
        sum_sent(TIME, t)
        sum_sent(SPACE, t)
    out_copy.wait()
    grad_copy.wait()


def hand_over(*refs):
    sources, targets, held, sems = refs[:6], refs[6:12], refs[12:18], refs[18]
    loads = [pltpu.make_async_copy(sources[i], held[i], sems.at[0, i]) for i in range(6)]
    stores = [pltpu.make_async_copy(held[i], targets[i], sems.at[1, i]) for i in range(6)]
    for load in loads:
        load.start()
    for load, store in zip(loads, stores):
        load.wait()
        store.start()
    for store in stores:
        store.wait()


def shards(video, w_qkv_space, w_out_space, w_qkv_time, w_out_time, grad_out):
    V = lambda *s: pltpu.VMEM(s, BF16)
    anywhere = pl.BlockSpec(memory_space=pl.ANY)
    vmem = pl.BlockSpec(memory_space=pltpu.VMEM)
    tokens = jax.ShapeDtypeStruct((ROWS, D), BF16)
    wide = jax.ShapeDtypeStruct((24, 3 * D), F32)
    narrow = jax.ShapeDtypeStruct((24, D), F32)
    outs = pl.pallas_call(
        kernel,
        out_shape=[tokens, tokens, wide, narrow, wide, narrow],
        in_specs=[anywhere] * 6,
        out_specs=[anywhere] * 2 + [vmem] * 4,
        scratch_shapes=[
            V(ROWS, D), V(ROWS, D), V(D, 3 * D), V(D, D), V(D, 3 * D), V(D, D),
            V(ROWS, 3 * D), V(ROWS, 3 * D), V(ROWS, D), V(ROWS, D), V(ROWS, 3 * D), V(ROWS, D),
            V(ROWS, D), V(ROWS, D), V(D, ROWS), V(D, ROWS), V(D, ROWS), V(D, ROWS),
            V(12, ROWS, ROWS), V(12, ROWS, 128), V(ROWS, ROWS), V(ROWS, ROWS), V(ROWS, D), V(ROWS, D), V(ROWS, D),
            V(4, GROUP, 16, 384), V(4, GROUP, 16, 384),
            V(2, 2, 2, 3, 4, 4, 2, 48, 128), V(2, 2, 3, 4, 4, 2, 48, 128), V(2, 2, 3, 3, 4, 2, 48, 128),
            V(2, 2, 3, 4, 2, 48, 128), V(2, 2, 3, 3, 2, 48, 128), V(2, 2, 3, 4, 32, 128), V(2, 2, 3, 3, 32, 128),
            V(2, 2, 3, 32, 128), V(2, 2, 3, 32, 128), V(2, 2, 3, 32, 128), V(2, 2, 3, 3, 32, 128),
            pltpu.SemaphoreType.DMA((8,)), pltpu.SemaphoreType.DMA((4,)), pltpu.SemaphoreType.DMA((4,)),
            pltpu.SemaphoreType.DMA((2, 2, 12)), pltpu.SemaphoreType.DMA((2, 2, 12)),
        ],
        compiler_params=pltpu.CompilerParams(
            collective_id=0, has_side_effects=True, vmem_limit_bytes=60 * 2**20
        ),
        name="layer",
    )(
        video.reshape(ROWS, D), w_qkv_space, w_out_space, w_qkv_time, w_out_time, grad_out.reshape(ROWS, D)
    )
    outs = pl.pallas_call(
        hand_over,
        out_shape=[jax.ShapeDtypeStruct(o.shape, o.dtype) for o in outs],
        in_specs=[anywhere] * 6,
        out_specs=[anywhere] * 6,
        scratch_shapes=[pltpu.VMEM(o.shape, o.dtype) for o in outs] + [pltpu.SemaphoreType.DMA((2, 6))],
        name="hand_over",
    )(*outs)
    shape = (1, 1, ROWS, D)
    return (outs[0].reshape(shape), outs[1].reshape(shape), outs[2], outs[3], outs[4], outs[5])


def solution(mesh):
    return jax.shard_map(
        shards,
        mesh=mesh,
        in_specs=(P("dp", "seq", None, None), P(), P(), P(), P(), P("dp", "seq", None, None)),
        out_specs=(
            P("dp", "seq", None, None),
            P("dp", "seq", None, None),
            P("seq", None),
            P("seq", None),
            P("seq", None),
            P("seq", None),
        ),
        check_vma=False,
    )
```

```python
import itertools
import math

import jax
import jax.numpy as jnp
from jax import lax
from jax.experimental import pallas as pl
from jax.experimental.pallas import tpu as pltpu
from jax.sharding import PartitionSpec as P

MESH = pl.DeviceIdType.MESH
F32 = jnp.float32
BF16 = jnp.bfloat16
HD = 64
D = 768
HALF = 384
ROWS = 256
PAIRS = 6
GROUP = 32
EPSILON = 1e-05
SCALE = 1.0 / math.sqrt(HD)
SCALE_LOG2E = SCALE * math.log2(math.e)
TIME, SPACE = 0, 1
ORDERS = (
    (("xyz", "yzx", "xzy"), ("xyz", "yzx", "yxz")),
    (("xyz", "yzx", "zxy"), ("xyz", "yzx", "zxy")),
)


def place(x, y, z, c):
    return ((z // 4) * 4 + y, (z % 4) * 8 + x * 2 + c)


def mm(a, b):
    return jnp.dot(a, b, preferred_element_type=F32)


def mm_nt(a, b):
    return lax.dot_general(a, b, (((1,), (1,)), ((), ())), preferred_element_type=F32)


def mm_tn(a, b):
    return lax.dot_general(a, b, (((0,), (0,)), ((), ())), preferred_element_type=F32)


def normalize(rows):
    mean = jnp.mean(rows, axis=-1, keepdims=True)
    centred = rows - mean
    variance = jnp.mean(centred * centred, axis=-1, keepdims=True)
    inverse = lax.rsqrt(variance + EPSILON)
    return centred * inverse, inverse


def normalize_back(rows, d_normed):
    normed, inverse = normalize(rows)
    d_centre = jnp.mean(d_normed, axis=-1, keepdims=True)
    d_spread = jnp.mean(d_normed * normed, axis=-1, keepdims=True)
    return inverse * (d_normed - d_centre - normed * d_spread)


def pack(rows):
    cut = rows.reshape(GROUP, 8, D)
    return jnp.concatenate([cut[:, :, : D // 2], cut[:, :, D // 2 :]], axis=1).astype(BF16)


def unpack(blocks):
    wide = blocks.astype(F32)
    return jnp.concatenate([wide[:, :8], wide[:, 8:]], axis=2).reshape(ROWS, D)


def softmax(scores):
    highest = jnp.max(scores, axis=-1, keepdims=True)
    weights = jnp.exp2((scores - highest) * SCALE_LOG2E)
    return weights * (1.0 / jnp.sum(weights, axis=-1, keepdims=True))


def kernel(
    video, wqs, wos, wqt, wot, gout,
    out_video, grad_video, oqs, oos, oqt, oot,
    vid_v, gout_v, wqs_v, wos_v, wqt_v, wot_v,
    qkv_s, qkv_t, att_s, att_t, dqkv, datt, tin, gt, nT, aT, nTs, aTs,
    probs_s, probs_t, bias, outv, gradv, d_space,
    sbuf, rbuf, G, r1, r2, b, r3, cc, r4, d, r5, e, f,
    lsem, asem, arsem, ssem, rsem,
):
    dp, seq = lax.axis_index("dp"), lax.axis_index("seq")
    x, y, z, c = (seq // 2) % 4, dp % 4, (dp // 4) * 4 + seq // 8, seq % 2
    tie = 1 - 2 * (z % 2)
    xs = [place((x + k) % 4, y, z, c) for k in (1, 2, 3)]
    ys = [place(x, (y + k) % 4, z, c) for k in (1, 2, 3)]
    zoff = [1, 7, (8 + 2 * tie) % 8]
    zt = [place(x, y, (z + o) % 8, c) for o in zoff]
    zs = [place(x, y, (z + 8 - o) % 8, c) for o in zoff]
    zh = place(x, y, (z + 4) % 8, c)
    core = place(x, y, z, 1 - c)
    targets = {
        "x": [(p, (x + k) % 4) for p, k in zip(xs, (1, 2, 3))],
        "y": [(p, (y + k) % 4) for p, k in zip(ys, (1, 2, 3))],
        "z": [(p, (z + o) % 4) for p, o in zip(zt, zoff)],
    }
    own = {"x": x, "y": y, "z": z % 4}

    loads = [
        pltpu.make_async_copy(src, dst, lsem.at[i])
        for i, (src, dst) in enumerate(
            ((video, vid_v), (wqs, wqs_v), (wos, wos_v), (gout, gout_v), (wqt, wqt_v), (wot, wot_v))
        )
    ]
    for i in (0, 3, 1, 2):
        loads[i].start()

    barrier = pltpu.get_barrier_semaphore()

    def greet(k, _):
        pl.semaphore_signal(barrier, inc=1, device_id=(dp, (seq + k) % GROUP), device_id_type=MESH)
        return 0

    lax.fori_loop(1, GROUP, greet, 0)
    for peer in ys + zs + [zh]:
        pl.semaphore_signal(barrier, inc=1, device_id=peer, device_id_type=MESH)

    def done(ref, sem):
        pltpu.make_async_copy(ref, ref, sem).wait()

    def exchange(i, first=1, last=GROUP):
        def one(k, _):
            far = GROUP - k
            to = ((seq // 8 + far // 8) % 4) * 8 + (x + far // 2) % 4 * 2 + (c + far) % 2
            pltpu.make_async_remote_copy(
                sbuf.at[i, to], rbuf.at[i, seq], asem.at[i], arsem.at[i],
                device_id=(dp, to), device_id_type=MESH,
            ).start()
            return 0

        lax.fori_loop(first, last, one, 0)
        if first == 1:
            rbuf[i, seq] = sbuf[i, seq]

    def left(i):
        done(rbuf.at[i, pl.ds(0, GROUP - 1)], asem.at[i])

    def arrived(i):
        done(rbuf.at[i, pl.ds(0, GROUP - 1)], arsem.at[i])

    def send(src, dst, h, t, s, dev):
        pltpu.make_async_remote_copy(
            src, dst, ssem.at[h, t, s], rsem.at[h, t, s], device_id=dev, device_id_type=MESH
        ).start()

    def sum_core_start(h, t):
        send(G.at[h, t, 1 - c], r1.at[h, t], h, t, 0, core)

    def sum_add(h, t):
        done(r1.at[h, t], rsem.at[h, t, 0])
        for j in range(3):
            def body(i, _):
                r1[h, t, j, i] = (G[h, t, c, j, i].astype(F32) + r1[h, t, j, i].astype(F32)).astype(BF16)
                return 0

            lax.fori_loop(0, 4, body, 0, unroll=True)

    def sum_first(h, t, thirds=(0, 1, 2)):
        for j in thirds:
            for k, (dev, o) in enumerate(targets[ORDERS[h][t][j][0]]):
                send(r1.at[h, t, j, o], r2.at[h, t, j, k], h, t, 1 + j, dev)

    def sum_second(h, t):
        for j in range(3):
            done(r2.at[h, t, j], rsem.at[h, t, 1 + j])
            o0 = own[ORDERS[h][t][j][0]]

            def body(i, _):
                total = r1[h, t, j, o0, i].astype(F32)
                for k in range(3):
                    total = total + r2[h, t, j, k, i].astype(F32)
                b[h, t, j, i] = total.astype(BF16)
                return 0

            lax.fori_loop(0, 4, body, 0, unroll=True)
            for k, (dev, o) in enumerate(targets[ORDERS[h][t][j][1]]):
                send(b.at[h, t, j, o], r3.at[h, t, j, k], h, t, 4 + j, dev)

    def sum_third(h, t):
        for j in range(3):
            done(r3.at[h, t, j], rsem.at[h, t, 4 + j])
            total = b[h, t, j, own[ORDERS[h][t][j][1]]].astype(F32)
            for k in range(3):
                total = total + r3[h, t, j, k].astype(F32)
            for o in range(4):
                piece = total[o // 2, 24 * (o % 2) : 24 * (o % 2) + 24]
                piece = jnp.concatenate([piece, jnp.zeros((8, 128), F32)], axis=0)
                cc[h, t, j, o] = piece.astype(BF16)
            for k, (dev, o) in enumerate(targets[ORDERS[h][t][j][2]]):
                send(cc.at[h, t, j, o], r4.at[h, t, j, k], h, t, 7 + j, dev)

    def sum_far(h, t):
        for j in range(3):
            done(r4.at[h, t, j], rsem.at[h, t, 7 + j])
            total = cc[h, t, j, own[ORDERS[h][t][j][2]]].astype(F32)
            for k in range(3):
                total = total + r4[h, t, j, k].astype(F32)
            d[h, t, j] = total.astype(BF16)
        send(d.at[h, t], r5.at[h, t], h, t, 10, zh)

    def sum_gather(h, t):
        done(r5.at[h, t], rsem.at[h, t, 10])
        e[h, t] = (d[h, t].astype(F32) + r5[h, t].astype(F32)).astype(BF16)
        for k, dev in enumerate(ys):
            send(e.at[h, t], f.at[h, t, k], h, t, 11, dev)

    def sum_finish(h, t, wide_out, narrow_out):
        done(f.at[h, t], rsem.at[h, t, 11])
        for k in range(4):
            block = (e[h, t] if k == 0 else f[h, t, k - 1]).astype(F32)
            source = (y + 4 - k) % 4
            for part in range(4):
                @pl.when(source == part)
                def _():
                    out, at = (wide_out, D * part) if part < 3 else (narrow_out, 0)
                    for j in range(3):
                        start = at + HALF * t + 128 * j
                        out[:, start : start + 128] = block[j, :24]

    def sum_sent(h, t):
        done(r1.at[h, t], ssem.at[h, t, 0])
        for j in range(3):
            done(r2.at[h, t, j], ssem.at[h, t, 1 + j])
            done(r3.at[h, t, j], ssem.at[h, t, 4 + j])
            done(r4.at[h, t, j], ssem.at[h, t, 7 + j])
        done(r5.at[h, t], ssem.at[h, t, 10])
        done(f.at[h, t], ssem.at[h, t, 11])

    def write_grad(h, t, left, left_out, d_out):
        right = jnp.concatenate([dqkv[:, D * part + HALF * t : D * part + HALF * t + HALF] for part in range(3)], axis=1)
        right_out = d_out[:, HALF * t : HALF * t + HALF]

        def body(zp, _):
            rows = pl.ds(pl.multiple_of(384 * zp, 128), 384)
            three = mm(left[rows, :], right)
            parts = [three[:, HALF * part : HALF * part + HALF] for part in range(3)] + [mm(left_out[rows, :], right_out)]

            def piece(part, z2, xp, cp, j):
                start = z2 * 192 + (xp * 2 + cp) * 24
                return parts[part][start : start + 24, 128 * j : 128 * j + 128]

            for j, order in enumerate(ORDERS[h][t]):
                last = order[2]
                spans = {"x": 4, "y": 4, "z": 2}
                spans[last] //= 2
                for xi, yi, zi, cp in itertools.product(*(range(spans[axis]) for axis in "xyz"), range(2)):
                    pair = []
                    for odd in range(2):
                        xp, part, z2 = xi, yi, zi
                        if last == "x":
                            xp = 2 * xi + odd
                        elif last == "y":
                            part = 2 * yi + odd
                        else:
                            z2 = odd
                        pair.append(piece(part, z2, xp, cp, j))
                    at = {"x": xi, "y": yi, "z": zp if last == "z" else 2 * zp + zi}
                    G[h, t, cp, j, at[order[0]], at[order[1]], at[last]] = jnp.concatenate(pair, axis=0).astype(BF16)
            return 0

        lax.fori_loop(0, 2, body, 0)

    left_half = lax.broadcasted_iota(jnp.int32, (1, 128), 1) < HD

    def halves(value):
        zero = jnp.zeros_like(value)
        return jnp.where(left_half, value, zero), jnp.where(left_half, zero, value)

    def columns(pair, part):
        return pl.ds(pl.multiple_of(part * D + pair * 128, 128), 128)

    def attend(qkv, probs, att, apart):
        def body(pair, _):
            queries = halves(qkv[:, columns(pair, 0)])
            keys = qkv[:, columns(pair, 1)]
            values = halves(qkv[:, columns(pair, 2)])
            total = 0.0
            for s in range(2):
                scores = mm_nt(queries[s], keys)
                if apart is not None:
                    scores = scores + apart[...]
                low = softmax(scores).astype(BF16)
                probs[pair * 2 + s] = low
                total = total + mm(low, values[s])
            att[:, columns(pair, 0)] = total.astype(BF16)
            return 0

        lax.fori_loop(0, PAIRS, body, 0, unroll=True)

    def attend_back(qkv, probs, first, last):
        def body(pair, _):
            queries = halves(qkv[:, columns(pair, 0)])
            keys = halves(qkv[:, columns(pair, 1)])
            values = qkv[:, columns(pair, 2)]
            d_out = halves(datt[:, columns(pair, 0)])
            d_queries = d_keys = d_values = 0.0
            for s in range(2):
                low = probs[pair * 2 + s]
                wide = low.astype(F32)
                product = mm_nt(d_out[s], values) * wide
                d_scores = (product - wide * jnp.sum(product, axis=-1, keepdims=True)).astype(BF16)
                d_values = d_values + mm_tn(low, d_out[s])
                d_queries = d_queries + mm(d_scores, keys[s])
                d_keys = d_keys + mm_tn(d_scores, queries[s])
            dqkv[:, columns(pair, 0)] = (d_queries * SCALE).astype(BF16)
            dqkv[:, columns(pair, 1)] = (d_keys * SCALE).astype(BF16)
            dqkv[:, columns(pair, 2)] = d_values.astype(BF16)
            return 0

        lax.fori_loop(first, last, body, 0, unroll=True)

    def project(normed, weights, qkv):
        for part in range(3):
            at = slice(part * D, part * D + D)
            qkv[:, at] = mm(normed, weights[:, at]).astype(BF16)

    def project_back(weights):
        total = mm_nt(dqkv[:, :D], weights[:, :D])
        for part in (1, 2):
            at = slice(part * D, part * D + D)
            total = total + mm_nt(dqkv[:, at], weights[:, at])
        return total

    loads[0].wait()
    normed = normalize(vid_v[...].astype(F32))[0].astype(BF16)
    loads[1].wait()
    loads[4].start()
    loads[5].start()
    project(normed, wqs_v, qkv_s)
    attend(qkv_s, probs_s, att_s, None)
    loads[2].wait()
    sbuf[1] = pack(vid_v[...].astype(F32) + mm(att_s[...], wos_v[...]))
    pl.semaphore_wait(barrier, GROUP - 1 + 7)
    exchange(1)
    loads[3].wait()
    sbuf[0] = pack(gout_v[...].astype(F32))

    ahead = lax.broadcasted_iota(jnp.int32, (ROWS, ROWS), 0) + (ROWS - lax.broadcasted_iota(jnp.int32, (ROWS, ROWS), 1))
    bias[...] = jnp.where(ahead % 8 == 0, 0.0, -1e30)
    nTs[...] = normalize(vid_v[...].astype(F32))[0].astype(BF16).T
    aTs[...] = att_s[...].T
    loads[4].wait()
    loads[5].wait()
    left(1)
    exchange(0)
    arrived(1)

    rows_in = unpack(rbuf[1])
    tin[...] = rows_in.astype(BF16)
    normed = normalize(rows_in)[0].astype(BF16)
    project(normed, wqt_v, qkv_t)
    attend(qkv_t, probs_t, att_t, bias)
    nT[...] = normed.T
    aT[...] = att_t[...].T
    sbuf[2] = pack(tin[...].astype(F32) + mm(att_t[...], wot_v[...]))
    arrived(0)
    gt[...] = unpack(rbuf[0]).astype(BF16)
    datt[...] = mm_nt(gt[...], wot_v[...]).astype(BF16)
    attend_back(qkv_t, probs_t, 0, PAIRS)
    d_rows = normalize_back(tin[...].astype(F32), project_back(wqt_v))
    sbuf[3] = pack(gt[...].astype(F32) + d_rows)
    exchange(3)
    for t in range(2):
        write_grad(TIME, t, nT, aT, gt)
        sum_core_start(TIME, t)
    for t in range(2):
        sum_add(TIME, t)
        sum_first(TIME, t)
    arrived(3)
    exchange(2)

    d_space[...] = unpack(rbuf[3]).astype(BF16)
    datt[...] = mm_nt(d_space[...], wos_v[...]).astype(BF16)
    attend_back(qkv_s, probs_s, 0, 3)
    write_grad(SPACE, 0, nTs, aTs, d_space)
    sum_core_start(SPACE, 0)
    attend_back(qkv_s, probs_s, 3, 6)
    write_grad(SPACE, 1, nTs, aTs, d_space)
    sum_core_start(SPACE, 1)
    sum_add(SPACE, 0)
    sum_first(SPACE, 0)
    d_rows = normalize_back(vid_v[...].astype(F32), project_back(wqs_v))
    gradv[...] = (d_space[...].astype(F32) + d_rows).astype(BF16)
    grad_copy = pltpu.make_async_copy(gradv, grad_video, lsem.at[7])
    grad_copy.start()
    sum_add(SPACE, 1)
    sum_first(SPACE, 1)
    sum_second(TIME, 0)
    sum_second(TIME, 1)
    arrived(2)
    outv[...] = unpack(rbuf[2]).astype(BF16)
    out_copy = pltpu.make_async_copy(outv, out_video, lsem.at[6])
    out_copy.start()
    sum_second(SPACE, 0)
    sum_third(TIME, 0)
    sum_third(TIME, 1)
    sum_second(SPACE, 1)
    sum_third(SPACE, 0)
    sum_far(TIME, 0)
    sum_far(TIME, 1)
    sum_third(SPACE, 1)
    sum_far(SPACE, 0)
    sum_gather(TIME, 0)
    sum_gather(TIME, 1)
    sum_far(SPACE, 1)
    sum_gather(SPACE, 0)
    sum_finish(TIME, 0, oqt, oot)
    sum_finish(TIME, 1, oqt, oot)
    sum_gather(SPACE, 1)
    sum_finish(SPACE, 0, oqs, oos)
    sum_finish(SPACE, 1, oqs, oos)
    for i in (0, 2, 3):
        left(i)
    for t in range(2):
        sum_sent(TIME, t)
        sum_sent(SPACE, t)
    out_copy.wait()
    grad_copy.wait()


def hand_over(*refs):
    sources, targets, held, sems = refs[:6], refs[6:12], refs[12:18], refs[18]
    loads = [pltpu.make_async_copy(sources[i], held[i], sems.at[0, i]) for i in range(6)]
    stores = [pltpu.make_async_copy(held[i], targets[i], sems.at[1, i]) for i in range(6)]
    for load in loads:
        load.start()
    for load, store in zip(loads, stores):
        load.wait()
        store.start()
    for store in stores:
        store.wait()


def shards(video, w_qkv_space, w_out_space, w_qkv_time, w_out_time, grad_out):
    V = lambda *s: pltpu.VMEM(s, BF16)
    anywhere = pl.BlockSpec(memory_space=pl.ANY)
    vmem = pl.BlockSpec(memory_space=pltpu.VMEM)
    tokens = jax.ShapeDtypeStruct((ROWS, D), BF16)
    wide = jax.ShapeDtypeStruct((24, 3 * D), F32)
    narrow = jax.ShapeDtypeStruct((24, D), F32)
    outs = pl.pallas_call(
        kernel,
        out_shape=[tokens, tokens, wide, narrow, wide, narrow],
        in_specs=[anywhere] * 6,
        out_specs=[anywhere] * 2 + [vmem] * 4,
        scratch_shapes=[
            V(ROWS, D), V(ROWS, D), V(D, 3 * D), V(D, D), V(D, 3 * D), V(D, D),
            V(ROWS, 3 * D), V(ROWS, 3 * D), V(ROWS, D), V(ROWS, D), V(ROWS, 3 * D), V(ROWS, D),
            V(ROWS, D), V(ROWS, D), V(D, ROWS), V(D, ROWS), V(D, ROWS), V(D, ROWS),
            V(12, ROWS, ROWS), V(12, ROWS, ROWS), pltpu.VMEM((ROWS, ROWS), F32), V(ROWS, D), V(ROWS, D), V(ROWS, D),
            V(4, GROUP, 16, 384), V(4, GROUP, 16, 384),
            V(2, 2, 2, 3, 4, 4, 2, 48, 128), V(2, 2, 3, 4, 4, 2, 48, 128), V(2, 2, 3, 3, 4, 2, 48, 128),
            V(2, 2, 3, 4, 2, 48, 128), V(2, 2, 3, 3, 2, 48, 128), V(2, 2, 3, 4, 32, 128), V(2, 2, 3, 3, 32, 128),
            V(2, 2, 3, 32, 128), V(2, 2, 3, 32, 128), V(2, 2, 3, 32, 128), V(2, 2, 3, 3, 32, 128),
            pltpu.SemaphoreType.DMA((8,)), pltpu.SemaphoreType.DMA((4,)), pltpu.SemaphoreType.DMA((4,)),
            pltpu.SemaphoreType.DMA((2, 2, 12)), pltpu.SemaphoreType.DMA((2, 2, 12)),
        ],
        compiler_params=pltpu.CompilerParams(
            collective_id=0, has_side_effects=True, vmem_limit_bytes=60 * 2**20
        ),
        name="layer",
    )(
        video.reshape(ROWS, D), w_qkv_space, w_out_space, w_qkv_time, w_out_time, grad_out.reshape(ROWS, D)
    )
    outs = pl.pallas_call(
        hand_over,
        out_shape=[jax.ShapeDtypeStruct(o.shape, o.dtype) for o in outs],
        in_specs=[anywhere] * 6,
        out_specs=[anywhere] * 6,
        scratch_shapes=[pltpu.VMEM(o.shape, o.dtype) for o in outs] + [pltpu.SemaphoreType.DMA((2, 6))],
        name="hand_over",
    )(*outs)
    shape = (1, 1, ROWS, D)
    return (outs[0].reshape(shape), outs[1].reshape(shape), outs[2], outs[3], outs[4], outs[5])


def solution(mesh):
    return jax.shard_map(
        shards,
        mesh=mesh,
        in_specs=(P("dp", "seq", None, None), P(), P(), P(), P(), P("dp", "seq", None, None)),
        out_specs=(
            P("dp", "seq", None, None),
            P("dp", "seq", None, None),
            P("seq", None),
            P("seq", None),
            P("seq", None),
            P("seq", None),
        ),
        check_vma=False,
    )
```

```python
import itertools
import math

import jax
import jax.numpy as jnp
from jax import lax
from jax.experimental import pallas as pl
from jax.experimental.pallas import tpu as pltpu
from jax.sharding import PartitionSpec as P

MESH = pl.DeviceIdType.MESH
F32 = jnp.float32
BF16 = jnp.bfloat16
HD = 64
D = 768
HALF = 384
ROWS = 256
PAIRS = 6
GROUP = 32
EPSILON = 1e-05
SCALE = 1.0 / math.sqrt(HD)
SCALE_LOG2E = SCALE * math.log2(math.e)
TIME, SPACE = 0, 1
ORDERS = (
    (("xyz", "yzx", "yxz"), ("xyz", "yzx", "zxy")),
    (("xyz", "yzx", "zxy"), ("xyz", "yzx", "zxy")),
)


def place(x, y, z, c):
    return ((z // 4) * 4 + y, (z % 4) * 8 + x * 2 + c)


def mm(a, b):
    return jnp.dot(a, b, preferred_element_type=F32)


def mm_nt(a, b):
    return lax.dot_general(a, b, (((1,), (1,)), ((), ())), preferred_element_type=F32)


def mm_tn(a, b):
    return lax.dot_general(a, b, (((0,), (0,)), ((), ())), preferred_element_type=F32)


def normalize(rows):
    mean = jnp.mean(rows, axis=-1, keepdims=True)
    centred = rows - mean
    variance = jnp.mean(centred * centred, axis=-1, keepdims=True)
    inverse = lax.rsqrt(variance + EPSILON)
    return centred * inverse, inverse


def normalize_back(rows, d_normed):
    normed, inverse = normalize(rows)
    d_centre = jnp.mean(d_normed, axis=-1, keepdims=True)
    d_spread = jnp.mean(d_normed * normed, axis=-1, keepdims=True)
    return inverse * (d_normed - d_centre - normed * d_spread)


def pack(rows):
    cut = rows.reshape(GROUP, 8, D)
    return jnp.concatenate([cut[:, :, : D // 2], cut[:, :, D // 2 :]], axis=1).astype(BF16)


def unpack(blocks):
    wide = blocks.astype(F32)
    return jnp.concatenate([wide[:, :8], wide[:, 8:]], axis=2).reshape(ROWS, D)


def softmax(scores):
    highest = jnp.max(scores, axis=-1, keepdims=True)
    weights = jnp.exp2((scores - highest) * SCALE_LOG2E)
    return weights * (1.0 / jnp.sum(weights, axis=-1, keepdims=True))


def kernel(
    video, wqs, wos, wqt, wot, gout,
    out_video, grad_video, oqs, oos, oqt, oot,
    vid_v, gout_v, wqs_v, wos_v, wqt_v, wot_v,
    qkv_s, qkv_t, att_s, att_t, dqkv, datt, tin, gt, nT, aT, nTs, aTs,
    probs_s, probs_t, bias, outv, gradv, d_space,
    sbuf, rbuf, G, r1, r2, b, r3, cc, r4, d, r5, e, f,
    lsem, asem, arsem, ssem, rsem,
):
    dp, seq = lax.axis_index("dp"), lax.axis_index("seq")
    x, y, z, c = (seq // 2) % 4, dp % 4, (dp // 4) * 4 + seq // 8, seq % 2
    tie = 1 - 2 * (z % 2)
    xs = [place((x + k) % 4, y, z, c) for k in (1, 2, 3)]
    ys = [place(x, (y + k) % 4, z, c) for k in (1, 2, 3)]
    zoff = [1, 7, (8 + 2 * tie) % 8]
    zt = [place(x, y, (z + o) % 8, c) for o in zoff]
    zs = [place(x, y, (z + 8 - o) % 8, c) for o in zoff]
    zh = place(x, y, (z + 4) % 8, c)
    core = place(x, y, z, 1 - c)
    targets = {
        "x": [(p, (x + k) % 4) for p, k in zip(xs, (1, 2, 3))],
        "y": [(p, (y + k) % 4) for p, k in zip(ys, (1, 2, 3))],
        "z": [(p, (z + o) % 4) for p, o in zip(zt, zoff)],
    }
    own = {"x": x, "y": y, "z": z % 4}

    loads = [
        pltpu.make_async_copy(src, dst, lsem.at[i])
        for i, (src, dst) in enumerate(
            ((video, vid_v), (wqs, wqs_v), (wos, wos_v), (gout, gout_v), (wqt, wqt_v), (wot, wot_v))
        )
    ]
    for i in (0, 3, 1, 2):
        loads[i].start()

    barrier = pltpu.get_barrier_semaphore()

    def greet(k, _):
        pl.semaphore_signal(barrier, inc=1, device_id=(dp, (seq + k) % GROUP), device_id_type=MESH)
        return 0

    lax.fori_loop(1, GROUP, greet, 0)
    for peer in ys + zs + [zh]:
        pl.semaphore_signal(barrier, inc=1, device_id=peer, device_id_type=MESH)

    def done(ref, sem):
        pltpu.make_async_copy(ref, ref, sem).wait()

    def exchange(i, first=1, last=GROUP):
        def one(k, _):
            far = GROUP - k
            to = ((seq // 8 + far // 8) % 4) * 8 + (x + far // 2) % 4 * 2 + (c + far) % 2
            pltpu.make_async_remote_copy(
                sbuf.at[i, to], rbuf.at[i, seq], asem.at[i], arsem.at[i],
                device_id=(dp, to), device_id_type=MESH,
            ).start()
            return 0

        lax.fori_loop(first, last, one, 0)
        if first == 1:
            rbuf[i, seq] = sbuf[i, seq]

    def left(i):
        done(rbuf.at[i, pl.ds(0, GROUP - 1)], asem.at[i])

    def arrived(i):
        done(rbuf.at[i, pl.ds(0, GROUP - 1)], arsem.at[i])

    def send(src, dst, h, t, s, dev):
        pltpu.make_async_remote_copy(
            src, dst, ssem.at[h, t, s], rsem.at[h, t, s], device_id=dev, device_id_type=MESH
        ).start()

    def sum_core_start(h, t):
        send(G.at[h, t, 1 - c], r1.at[h, t], h, t, 0, core)

    def sum_add(h, t):
        done(r1.at[h, t], rsem.at[h, t, 0])
        for j in range(3):
            def body(i, _):
                r1[h, t, j, i] = (G[h, t, c, j, i].astype(F32) + r1[h, t, j, i].astype(F32)).astype(BF16)
                return 0

            lax.fori_loop(0, 4, body, 0, unroll=True)

    def sum_first(h, t, thirds=(0, 1, 2)):
        for j in thirds:
            for k, (dev, o) in enumerate(targets[ORDERS[h][t][j][0]]):
                send(r1.at[h, t, j, o], r2.at[h, t, j, k], h, t, 1 + j, dev)

    def sum_second(h, t):
        for j in range(3):
            done(r2.at[h, t, j], rsem.at[h, t, 1 + j])
            o0 = own[ORDERS[h][t][j][0]]

            def body(i, _):
                total = r1[h, t, j, o0, i].astype(F32)
                for k in range(3):
                    total = total + r2[h, t, j, k, i].astype(F32)
                b[h, t, j, i] = total.astype(BF16)
                return 0

            lax.fori_loop(0, 4, body, 0, unroll=True)
            for k, (dev, o) in enumerate(targets[ORDERS[h][t][j][1]]):
                send(b.at[h, t, j, o], r3.at[h, t, j, k], h, t, 4 + j, dev)

    def sum_third(h, t):
        for j in range(3):
            done(r3.at[h, t, j], rsem.at[h, t, 4 + j])
            total = b[h, t, j, own[ORDERS[h][t][j][1]]].astype(F32)
            for k in range(3):
                total = total + r3[h, t, j, k].astype(F32)
            for o in range(4):
                piece = total[o // 2, 24 * (o % 2) : 24 * (o % 2) + 24]
                piece = jnp.concatenate([piece, jnp.zeros((8, 128), F32)], axis=0)
                cc[h, t, j, o] = piece.astype(BF16)
            for k, (dev, o) in enumerate(targets[ORDERS[h][t][j][2]]):
                send(cc.at[h, t, j, o], r4.at[h, t, j, k], h, t, 7 + j, dev)

    def sum_far(h, t):
        for j in range(3):
            done(r4.at[h, t, j], rsem.at[h, t, 7 + j])
            total = cc[h, t, j, own[ORDERS[h][t][j][2]]].astype(F32)
            for k in range(3):
                total = total + r4[h, t, j, k].astype(F32)
            d[h, t, j] = total.astype(BF16)
        send(d.at[h, t], r5.at[h, t], h, t, 10, zh)

    def sum_gather(h, t):
        done(r5.at[h, t], rsem.at[h, t, 10])
        e[h, t] = (d[h, t].astype(F32) + r5[h, t].astype(F32)).astype(BF16)
        for k, dev in enumerate(ys):
            send(e.at[h, t], f.at[h, t, k], h, t, 11, dev)

    def sum_finish(h, t, wide_out, narrow_out):
        done(f.at[h, t], rsem.at[h, t, 11])
        for k in range(4):
            block = (e[h, t] if k == 0 else f[h, t, k - 1]).astype(F32)
            source = (y + 4 - k) % 4
            for part in range(4):
                @pl.when(source == part)
                def _():
                    out, at = (wide_out, D * part) if part < 3 else (narrow_out, 0)
                    for j in range(3):
                        start = at + HALF * t + 128 * j
                        out[:, start : start + 128] = block[j, :24]

    def sum_sent(h, t):
        done(r1.at[h, t], ssem.at[h, t, 0])
        for j in range(3):
            done(r2.at[h, t, j], ssem.at[h, t, 1 + j])
            done(r3.at[h, t, j], ssem.at[h, t, 4 + j])
            done(r4.at[h, t, j], ssem.at[h, t, 7 + j])
        done(r5.at[h, t], ssem.at[h, t, 10])
        done(f.at[h, t], ssem.at[h, t, 11])

    def write_grad(h, t, left, left_out, d_out):
        right = jnp.concatenate([dqkv[:, D * part + HALF * t : D * part + HALF * t + HALF] for part in range(3)], axis=1)
        right_out = d_out[:, HALF * t : HALF * t + HALF]

        def body(zp, _):
            rows = pl.ds(pl.multiple_of(384 * zp, 128), 384)
            three = mm(left[rows, :], right)
            parts = [three[:, HALF * part : HALF * part + HALF] for part in range(3)] + [mm(left_out[rows, :], right_out)]

            def piece(part, z2, xp, cp, j):
                start = z2 * 192 + (xp * 2 + cp) * 24
                return parts[part][start : start + 24, 128 * j : 128 * j + 128]

            for j, order in enumerate(ORDERS[h][t]):
                last = order[2]
                spans = {"x": 4, "y": 4, "z": 2}
                spans[last] //= 2
                for xi, yi, zi, cp in itertools.product(*(range(spans[axis]) for axis in "xyz"), range(2)):
                    pair = []
                    for odd in range(2):
                        xp, part, z2 = xi, yi, zi
                        if last == "x":
                            xp = 2 * xi + odd
                        elif last == "y":
                            part = 2 * yi + odd
                        else:
                            z2 = odd
                        pair.append(piece(part, z2, xp, cp, j))
                    at = {"x": xi, "y": yi, "z": zp if last == "z" else 2 * zp + zi}
                    G[h, t, cp, j, at[order[0]], at[order[1]], at[last]] = jnp.concatenate(pair, axis=0).astype(BF16)
            return 0

        lax.fori_loop(0, 2, body, 0)

    left_half = lax.broadcasted_iota(jnp.int32, (1, 128), 1) < HD

    def halves(value):
        zero = jnp.zeros_like(value)
        return jnp.where(left_half, value, zero), jnp.where(left_half, zero, value)

    def columns(pair, part):
        return pl.ds(pl.multiple_of(part * D + pair * 128, 128), 128)

    def attend(qkv, probs, att, apart):
        def body(pair, _):
            queries = halves(qkv[:, columns(pair, 0)])
            keys = qkv[:, columns(pair, 1)]
            values = halves(qkv[:, columns(pair, 2)])
            total = 0.0
            for s in range(2):
                scores = mm_nt(queries[s], keys)
                if apart is not None:
                    scores = scores + apart[...]
                low = softmax(scores).astype(BF16)
                probs[pair * 2 + s] = low
                total = total + mm(low, values[s])
            att[:, columns(pair, 0)] = total.astype(BF16)
            return 0

        lax.fori_loop(0, PAIRS, body, 0, unroll=True)

    def attend_back(qkv, probs, first, last):
        def body(pair, _):
            queries = halves(qkv[:, columns(pair, 0)])
            keys = halves(qkv[:, columns(pair, 1)])
            values = qkv[:, columns(pair, 2)]
            d_out = halves(datt[:, columns(pair, 0)])
            d_queries = d_keys = d_values = 0.0
            for s in range(2):
                low = probs[pair * 2 + s]
                wide = low.astype(F32)
                product = mm_nt(d_out[s], values) * wide
                d_scores = (product - wide * jnp.sum(product, axis=-1, keepdims=True)).astype(BF16)
                d_values = d_values + mm_tn(low, d_out[s])
                d_queries = d_queries + mm(d_scores, keys[s])
                d_keys = d_keys + mm_tn(d_scores, queries[s])
            dqkv[:, columns(pair, 0)] = (d_queries * SCALE).astype(BF16)
            dqkv[:, columns(pair, 1)] = (d_keys * SCALE).astype(BF16)
            dqkv[:, columns(pair, 2)] = d_values.astype(BF16)
            return 0

        lax.fori_loop(first, last, body, 0, unroll=True)

    def project(normed, weights, qkv):
        for part in range(3):
            at = slice(part * D, part * D + D)
            qkv[:, at] = mm(normed, weights[:, at]).astype(BF16)

    def project_back(weights):
        total = mm_nt(dqkv[:, :D], weights[:, :D])
        for part in (1, 2):
            at = slice(part * D, part * D + D)
            total = total + mm_nt(dqkv[:, at], weights[:, at])
        return total

    loads[0].wait()
    normed = normalize(vid_v[...].astype(F32))[0].astype(BF16)
    loads[1].wait()
    loads[4].start()
    loads[5].start()
    project(normed, wqs_v, qkv_s)
    attend(qkv_s, probs_s, att_s, None)
    loads[2].wait()
    sbuf[1] = pack(vid_v[...].astype(F32) + mm(att_s[...], wos_v[...]))
    pl.semaphore_wait(barrier, GROUP - 1 + 7)
    exchange(1)
    loads[3].wait()
    sbuf[0] = pack(gout_v[...].astype(F32))

    ahead = lax.broadcasted_iota(jnp.int32, (ROWS, ROWS), 0) + (ROWS - lax.broadcasted_iota(jnp.int32, (ROWS, ROWS), 1))
    bias[...] = jnp.where(ahead % 8 == 0, 0.0, -1e30)
    nTs[...] = normalize(vid_v[...].astype(F32))[0].astype(BF16).T
    aTs[...] = att_s[...].T
    loads[4].wait()
    loads[5].wait()
    left(1)
    exchange(0)
    arrived(1)

    rows_in = unpack(rbuf[1])
    tin[...] = rows_in.astype(BF16)
    normed = normalize(rows_in)[0].astype(BF16)
    project(normed, wqt_v, qkv_t)
    attend(qkv_t, probs_t, att_t, bias)
    nT[...] = normed.T
    aT[...] = att_t[...].T
    sbuf[2] = pack(tin[...].astype(F32) + mm(att_t[...], wot_v[...]))
    arrived(0)
    gt[...] = unpack(rbuf[0]).astype(BF16)
    datt[...] = mm_nt(gt[...], wot_v[...]).astype(BF16)
    attend_back(qkv_t, probs_t, 0, PAIRS)
    d_rows = normalize_back(tin[...].astype(F32), project_back(wqt_v))
    sbuf[3] = pack(gt[...].astype(F32) + d_rows)
    exchange(3)
    for t in range(2):
        write_grad(TIME, t, nT, aT, gt)
        sum_core_start(TIME, t)
    for t in range(2):
        sum_add(TIME, t)
        sum_first(TIME, t, (0, 1, 2)[: 3 - t])
    arrived(3)
    sum_first(TIME, 1, (2,))
    exchange(2)

    d_space[...] = unpack(rbuf[3]).astype(BF16)
    datt[...] = mm_nt(d_space[...], wos_v[...]).astype(BF16)
    attend_back(qkv_s, probs_s, 0, 3)
    write_grad(SPACE, 0, nTs, aTs, d_space)
    sum_core_start(SPACE, 0)
    attend_back(qkv_s, probs_s, 3, 6)
    write_grad(SPACE, 1, nTs, aTs, d_space)
    sum_core_start(SPACE, 1)
    sum_add(SPACE, 0)
    sum_first(SPACE, 0)
    d_rows = normalize_back(vid_v[...].astype(F32), project_back(wqs_v))
    gradv[...] = (d_space[...].astype(F32) + d_rows).astype(BF16)
    grad_copy = pltpu.make_async_copy(gradv, grad_video, lsem.at[7])
    grad_copy.start()
    sum_add(SPACE, 1)
    sum_first(SPACE, 1)
    arrived(2)
    outv[...] = unpack(rbuf[2]).astype(BF16)
    out_copy = pltpu.make_async_copy(outv, out_video, lsem.at[6])
    out_copy.start()
    sum_second(SPACE, 0)
    sum_second(TIME, 0)
    sum_second(TIME, 1)
    sum_second(SPACE, 1)
    sum_third(SPACE, 0)
    sum_third(TIME, 0)
    sum_third(TIME, 1)
    sum_third(SPACE, 1)
    sum_far(SPACE, 0)
    sum_far(TIME, 0)
    sum_far(TIME, 1)
    sum_far(SPACE, 1)
    sum_gather(SPACE, 0)
    sum_gather(TIME, 0)
    sum_gather(TIME, 1)
    sum_gather(SPACE, 1)
    sum_finish(SPACE, 0, oqs, oos)
    sum_finish(TIME, 0, oqt, oot)
    sum_finish(TIME, 1, oqt, oot)
    sum_finish(SPACE, 1, oqs, oos)
    for i in (0, 2, 3):
        left(i)
    for t in range(2):
        sum_sent(TIME, t)
        sum_sent(SPACE, t)
    out_copy.wait()
    grad_copy.wait()


def hand_over(*refs):
    sources, targets, held, sems = refs[:6], refs[6:12], refs[12:18], refs[18]
    loads = [pltpu.make_async_copy(sources[i], held[i], sems.at[0, i]) for i in range(6)]
    stores = [pltpu.make_async_copy(held[i], targets[i], sems.at[1, i]) for i in range(6)]
    for load in loads:
        load.start()
    for load, store in zip(loads, stores):
        load.wait()
        store.start()
    for store in stores:
        store.wait()


def shards(video, w_qkv_space, w_out_space, w_qkv_time, w_out_time, grad_out):
    V = lambda *s: pltpu.VMEM(s, BF16)
    anywhere = pl.BlockSpec(memory_space=pl.ANY)
    vmem = pl.BlockSpec(memory_space=pltpu.VMEM)
    tokens = jax.ShapeDtypeStruct((ROWS, D), BF16)
    wide = jax.ShapeDtypeStruct((24, 3 * D), F32)
    narrow = jax.ShapeDtypeStruct((24, D), F32)
    outs = pl.pallas_call(
        kernel,
        out_shape=[tokens, tokens, wide, narrow, wide, narrow],
        in_specs=[anywhere] * 6,
        out_specs=[anywhere] * 2 + [vmem] * 4,
        scratch_shapes=[
            V(ROWS, D), V(ROWS, D), V(D, 3 * D), V(D, D), V(D, 3 * D), V(D, D),
            V(ROWS, 3 * D), V(ROWS, 3 * D), V(ROWS, D), V(ROWS, D), V(ROWS, 3 * D), V(ROWS, D),
            V(ROWS, D), V(ROWS, D), V(D, ROWS), V(D, ROWS), V(D, ROWS), V(D, ROWS),
            V(12, ROWS, ROWS), V(12, ROWS, ROWS), pltpu.VMEM((ROWS, ROWS), F32), V(ROWS, D), V(ROWS, D), V(ROWS, D),
            V(4, GROUP, 16, 384), V(4, GROUP, 16, 384),
            V(2, 2, 2, 3, 4, 4, 2, 48, 128), V(2, 2, 3, 4, 4, 2, 48, 128), V(2, 2, 3, 3, 4, 2, 48, 128),
            V(2, 2, 3, 4, 2, 48, 128), V(2, 2, 3, 3, 2, 48, 128), V(2, 2, 3, 4, 32, 128), V(2, 2, 3, 3, 32, 128),
            V(2, 2, 3, 32, 128), V(2, 2, 3, 32, 128), V(2, 2, 3, 32, 128), V(2, 2, 3, 3, 32, 128),
            pltpu.SemaphoreType.DMA((8,)), pltpu.SemaphoreType.DMA((4,)), pltpu.SemaphoreType.DMA((4,)),
            pltpu.SemaphoreType.DMA((2, 2, 12)), pltpu.SemaphoreType.DMA((2, 2, 12)),
        ],
        compiler_params=pltpu.CompilerParams(
            collective_id=0, has_side_effects=True, vmem_limit_bytes=60 * 2**20
        ),
        name="layer",
    )(
        video.reshape(ROWS, D), w_qkv_space, w_out_space, w_qkv_time, w_out_time, grad_out.reshape(ROWS, D)
    )
    outs = pl.pallas_call(
        hand_over,
        out_shape=[jax.ShapeDtypeStruct(o.shape, o.dtype) for o in outs],
        in_specs=[anywhere] * 6,
        out_specs=[anywhere] * 6,
        scratch_shapes=[pltpu.VMEM(o.shape, o.dtype) for o in outs] + [pltpu.SemaphoreType.DMA((2, 6))],
        name="hand_over",
    )(*outs)
    shape = (1, 1, ROWS, D)
    return (outs[0].reshape(shape), outs[1].reshape(shape), outs[2], outs[3], outs[4], outs[5])


def solution(mesh):
    return jax.shard_map(
        shards,
        mesh=mesh,
        in_specs=(P("dp", "seq", None, None), P(), P(), P(), P(), P("dp", "seq", None, None)),
        out_specs=(
            P("dp", "seq", None, None),
            P("dp", "seq", None, None),
            P("seq", None),
            P("seq", None),
            P("seq", None),
            P("seq", None),
        ),
        check_vma=False,
    )
```
